512 devices in a mesh: head: 8 (over y_lo, x), seq: 64 (over z, y_hi, core).
Axes of the slice: x: 4, y: 8 (y_hi: 4, y_lo: 2; y = y_hi * 2 + y_lo), z: 8, core: 2. Of those that a mesh axis runs over, the one named last changes fastest.
Arguments:
- hidden: bfloat16 [2048, 5120], P('seq', 'head'), may hold values from -6 to 6
- query: bfloat16 [2048, 3072], P('seq', 'head'), may hold values from -1000 to 1000
- key: bfloat16 [2048, 3072], P('seq', 'head'), may hold values from -1000 to 1000
- value: bfloat16 [2048, 3072], P('seq', 'head'), may hold values from -8 to 8
- query_gain: float32 [3072], P('head'), may hold values from 0.5 to 3
- key_gain: float32 [3072], P('head'), may hold values from 0.5 to 3
- ref_key: bfloat16 [2048, 3072], P('seq', 'head'), may hold values from -8 to 8
- ref_value: bfloat16 [2048, 3072], P('seq', 'head'), may hold values from -8 to 8
- ref_count: int32 [64], P('seq'), may hold values from 1 to 32, 1024 in all
- out_weight: bfloat16 [3072, 5120], P('head'), may hold values from -0.109375 to 0.109375
- gate_table: float32 [50, 5120], P(None, 'head'), may hold values from -8 to 8
- frame_step: int32 [64], P('seq'), may hold values from 0 to 49
Outputs:
- updated: bfloat16 [2048, 5120], P('seq', 'head')
The draws below stay inside these ranges and needn't reach their ends.
Inputs may be any that keep to these rules, and one draw needn't show every extreme that they name: ref_count[p] counts the live slots of cycle position p, the first ones of its 32; the counts sum to 1024, and some position has all 32 slots live.
All inputs are finite; a program needn't handle non-finite values. No bound on the sum of `ref_count` on one device may be relied on, other than what follows from the above.
Results may differ from the reference program's by a relative error of at most 0.019.
Values may be sent and summed in bfloat16 or wider, within the bound.
No kernel may reach another device: no remote copies, remote signals or barrier semaphores. Data moves between devices by JAX's collectives and lax.ppermute only.
A program may use at most 64 MiB of HBM per device.

```python
import math
import jax
import jax.numpy as jnp
import numpy as np
from jax import lax

WIDTH = 5120
HEAD_DIM = 128
FRAME_TOK = 32
REF_SLOTS = 32
SAMPLE_STEPS = 50
FEATURES = 3072
CLIP_TOKENS = 2048
REF_ROWS = 2048
REF_TOTAL = 1024
FRAMES = 64
N_SEQ = 64


def scaled_field(seed_key):
    noise = jnp.clip(jax.random.normal(jax.random.fold_in(seed_key, 101), (CLIP_TOKENS, FEATURES), jnp.float32), -4.0, 4.0)
    row_scale = jnp.exp(jax.random.uniform(jax.random.fold_in(seed_key, 102), (CLIP_TOKENS, 1), jnp.float32, 0.0, math.log(10.0)))
    col_scale = jnp.exp(jax.random.uniform(jax.random.fold_in(seed_key, 103), (1, FEATURES), jnp.float32, 0.0, math.log(10.0)))
    ramp = jnp.exp(math.log(3.0) * jnp.arange(FEATURES, dtype=jnp.float32) / FEATURES)[None, :]
    return noise * row_scale * col_scale * ramp


def draw_key(key, part):
    base = scaled_field(key)
    return jnp.clip(base, -1000.0, 1000.0).astype(jnp.bfloat16)


def draw_query(key, part):
    key = jax.random.fold_in(key, 9)
    own_field = scaled_field(key)
    return jnp.clip(own_field, -1000.0, 1000.0).astype(jnp.bfloat16)


def draw_query_gain(key, part):
    key = jax.random.fold_in(key, 21)
    result = jnp.exp(jax.random.uniform(key, (FEATURES,), jnp.float32, math.log(0.5), math.log(1.5)))
    return result


def draw_key_gain(key, part):
    key = jax.random.fold_in(key, 23)
    result = jnp.exp(jax.random.uniform(key, (FEATURES,), jnp.float32, math.log(0.5), math.log(1.5)))
    return result


def place_ends(values, rng, smallest, high):
    place = [jax.random.randint(jax.random.fold_in(rng, axis), (), 0, length) for axis, length in enumerate(values.shape)]
    widest = values.shape.index(max(values.shape))
    next_to = place[:widest] + [(place[widest] + 1) % values.shape[widest]] + place[widest + 1:]
    return values.at[tuple(place)].set(smallest).at[tuple(next_to)].set(high)


def level_of(key, dims, shards, low, largest):
    loudness = 1.0
    for dim, blocks in shards:
        draws = jax.random.uniform(jax.random.fold_in(jax.random.fold_in(key, 6), dim), (blocks,), jnp.float32, low / len(shards), largest / len(shards))
        loudness = loudness * jnp.repeat(jnp.exp(draws), dims[dim] // blocks).reshape((-1,) + (1,) * (len(dims) - 1 - dim))
    return loudness


def profile(number_of, total, reach, skew):
    loads = [(1 << 20) // math.isqrt(grade ** skew) + 1 for grade in range(2, number_of + 1)]
    rest, counts = total - reach - (number_of - 1), [1] * (number_of - 1)
    while rest > 0:
        free = [i for i in range(number_of - 1) if counts[i] < reach]
        mass, budget = sum([loads[i] for i in free]), rest
        for i in free:
            addition = min(reach - counts[i], max(1, budget * loads[i] // mass), rest)
            counts[i] = counts[i] + addition
            rest = rest - addition
    return np.array([reach] + counts)


def ragged_sizes(stream_key, count, total, most, skew):
    if count == 2:
        one = jax.random.randint(stream_key, (), max(1, total - most), min(most, total - 1) + 1)
        return jnp.stack([one, total - one])
    sizes = jnp.asarray(profile(count, total, most, skew), jnp.int32)
    twos = (count - 1) // 2
    giver, receiver = sizes[1:1 + 2 * twos:2], sizes[2:2 + 2 * twos:2]
    room = jnp.minimum(giver - 1, most - receiver)
    shifted = jax.random.randint(jax.random.fold_in(stream_key, 1), (twos,), 0, 1 << 20) % (room + 1)
    sizes = sizes.at[1:1 + 2 * twos:2].set(giver - shifted).at[2:2 + 2 * twos:2].set(receiver + shifted)
    return sizes[jax.random.permutation(jax.random.fold_in(stream_key, 2), count)]


def normal_values(key, extent, width, limit, cuts=(), kind=jnp.bfloat16):
    drawn = jax.random.normal(key, extent, jnp.float32) * width
    if len(cuts) > 0:
        drawn = level_of(key, extent, cuts, -0.22, 0.18) * drawn
    return jnp.clip(drawn, min=-limit, max=limit).astype(kind)


def setup_inputs(seed: int = 0) -> dict:
    key_list = jax.random.split(jax.random.key(seed), 13)
    return {
        "hidden": normal_values(key_list[0], (CLIP_TOKENS, WIDTH), 1.0, 6.0, ((0, 64), (1, 8))),
        "query": draw_query(jax.random.fold_in(key_list[12], 71), 0),
        "key": draw_key(jax.random.fold_in(key_list[12], 71), 0),
        "value": normal_values(key_list[3], (CLIP_TOKENS, FEATURES), 2.0, 8.0, ((0, 64), (1, 8))),
        "query_gain": draw_query_gain(jax.random.fold_in(key_list[12], 71), 0),
        "key_gain": draw_key_gain(jax.random.fold_in(key_list[12], 71), 0),
        "ref_key": normal_values(key_list[6], (REF_ROWS, FEATURES), 1.5, 8.0, ((0, 64), (1, 8))),
        "ref_value": normal_values(key_list[7], (REF_ROWS, FEATURES), 2.0, 8.0, ((0, 64), (1, 8))),
        "ref_count": ragged_sizes(key_list[8], N_SEQ, REF_TOTAL, REF_SLOTS, 2).astype(jnp.int32),
        "out_weight": normal_values(key_list[9], (FEATURES, WIDTH), FEATURES ** -0.5, 0.109375, ((0, 8),)),
        "gate_table": normal_values(key_list[10], (SAMPLE_STEPS, WIDTH), 2.0, 8.0, ((1, 8),), jnp.float32),
        "frame_step": place_ends(jax.random.randint(key_list[11], (FRAMES,), 0, SAMPLE_STEPS), jax.random.fold_in(key_list[11], 1), 0, SAMPLE_STEPS - 1).astype(jnp.int32),
    }


EPSILON = 1e-06

def normed(projections, gain_row):
    widened = projections.astype(jnp.float32)
    mean_square = lax.optimization_barrier(jnp.mean(widened * widened, axis=1, keepdims=True))
    scaled = widened * lax.rsqrt(mean_square + EPSILON) * gain_row[None, :]
    return lax.optimization_barrier(scaled.astype(jnp.bfloat16))

def reference(hidden, query, key, value, query_gain, key_gain, ref_key, ref_value, ref_count, out_weight, gate_table, frame_step):
    head_count = FEATURES // HEAD_DIM
    query_norm = normed(query, query_gain)
    key_norm = normed(key, key_gain)
    slot_index = jnp.arange(REF_ROWS, dtype=jnp.int32)
    live_ref = slot_index % REF_SLOTS < ref_count[slot_index // REF_SLOTS]
    live_keys = jnp.concatenate([jnp.ones((CLIP_TOKENS,), jnp.bool_), live_ref])
    key_all = jnp.concatenate([key_norm, ref_key], axis=0).astype(jnp.float32)
    value_all = jnp.concatenate([value, ref_value], axis=0).astype(jnp.float32)
    key_heads = key_all.reshape(-1, head_count, HEAD_DIM).transpose(1, 0, 2)
    value_heads = value_all.reshape(-1, head_count, HEAD_DIM).transpose(1, 0, 2)
    query_heads = query_norm.astype(jnp.float32).reshape(CLIP_TOKENS, head_count, HEAD_DIM).transpose(1, 0, 2)
    block_rows = math.gcd(CLIP_TOKENS, 512)
    score_scale = 1.0 / math.sqrt(HEAD_DIM)

    def per_head(operands):
        head_query, head_keys, head_values = operands

        def per_block(query_block):
            scores = jnp.dot(query_block, head_keys.T, precision=lax.Precision.HIGHEST) * score_scale
            scores = jnp.where(live_keys[None, :], scores, -jnp.inf)
            row_max = lax.optimization_barrier(jnp.max(scores, axis=1, keepdims=True))
            weights = jnp.where(live_keys[None, :], jnp.exp(scores - row_max), 0.0)
            row_total = lax.optimization_barrier(jnp.sum(weights, axis=1, keepdims=True))
            rounded = lax.optimization_barrier(weights.astype(jnp.bfloat16)).astype(jnp.float32)
            return jnp.dot(rounded, head_values, precision=lax.Precision.HIGHEST) / row_total
        blocks = lax.map(per_block, head_query.reshape(-1, block_rows, HEAD_DIM))
        return blocks.reshape(CLIP_TOKENS, HEAD_DIM)
    head_outputs = lax.map(per_head, (query_heads, key_heads, value_heads))
    attended = head_outputs.transpose(1, 0, 2).reshape(CLIP_TOKENS, FEATURES).astype(jnp.bfloat16)
    projected = jnp.dot(attended, out_weight, preferred_element_type=jnp.float32)
    gate_rows = gate_table[jnp.repeat(frame_step, FRAME_TOK)]
    return (hidden.astype(jnp.float32) + gate_rows * projected).astype(jnp.bfloat16)
```

```python
import math

import jax
import jax.numpy as jnp
from jax import lax
from jax.experimental import pallas as pl
from jax.experimental.pallas import tpu as pltpu
from jax.sharding import Mesh
from jax.sharding import PartitionSpec as P

HEAD_DIM = 128
HEADS = 3
FEAT = HEADS * HEAD_DIM
ROWS = 32
WIDTH = 640
ALL_FEATURES = 3072
EPSILON = 1e-06
NEGATIVE = -1e30
SCALE = 1.0 / math.sqrt(HEAD_DIM)
BF = jnp.bfloat16
F32 = jnp.float32

HEAD_AXES = ("yl", "x")
SEQ_AXES = ("z", "yh", "c")
KEY_AXES = ("yh", "c")
QUERY_AXES = "z"
QB = 8
KB = 8
HB = 8


def call(kernel, out_shape, *args, in_specs=None):
    return pl.pallas_call(
        kernel,
        out_shape=out_shape,
        in_specs=in_specs or [pl.BlockSpec(memory_space=pltpu.VMEM)] * len(args),
        out_specs=pl.BlockSpec(memory_space=pltpu.VMEM),
        compiler_params=pltpu.CompilerParams(vmem_limit_bytes=24 * 1024 * 1024),
    )(*args)


def token_power(rows):
    wide = rows.astype(F32)
    squares = wide * wide
    part = squares[:, :128] + squares[:, 128:256] + squares[:, 256:]
    return jnp.sum(part.T, axis=0, keepdims=True)


def power_kernel(q_ref, kv_ref, out_ref):
    lines = []
    for g in range(2):
        lines.append(token_power(q_ref[g * 4 : g * 4 + 4].reshape(128, FEAT)))
    for g in range(2):
        lines.append(token_power(kv_ref[g * 4 : g * 4 + 4, :, :FEAT].reshape(128, FEAT)))
    block = jnp.concatenate(lines + [jnp.zeros((4, 128), F32)], axis=0)
    for peer in range(HB):
        out_ref[peer] = block


def attend_kernel(q_ref, kv_ref, pw_ref, gq_ref, gk_ref, out_ref):
    power = jnp.sum(pw_ref[...], axis=0) / ALL_FEATURES
    inverse = lax.rsqrt(power + EPSILON)

    def columns(first):
        tiles = [
            jnp.broadcast_to(inverse[first + g : first + g + 1], (128, 128)).T for g in range(2)
        ]
        return jnp.concatenate(tiles, axis=0)

    inv_q = columns(0)
    inv_k = columns(2)
    n_keys = KB * ROWS
    slot = lax.broadcasted_iota(jnp.int32, (1, n_keys), 1)
    counts = jnp.zeros((1, n_keys), F32)
    for p in range(KB):
        line = kv_ref[p, 0:16, 4 * FEAT :][0:1].astype(F32)
        counts = jnp.where(slot // ROWS == p, jnp.concatenate([line, line], axis=1), counts)
    live = (slot % ROWS).astype(F32) < counts
    lane = lax.broadcasted_iota(jnp.int32, (QB * ROWS, 128), 1)
    stats = jnp.zeros((QB * ROWS, 128), F32)
    contract = (((1,), (1,)), ((), ()))
    for h in range(HEADS):
        cols = slice(h * HEAD_DIM, (h + 1) * HEAD_DIM)

        def part(t):
            return kv_ref[:, :, t * FEAT + h * HEAD_DIM : t * FEAT + (h + 1) * HEAD_DIM].reshape(
                n_keys, HEAD_DIM
            )

        q = q_ref[:, :, cols].reshape(QB * ROWS, HEAD_DIM).astype(F32)
        q = (q * inv_q * gq_ref[:, cols]).astype(BF)
        k = (part(0).astype(F32) * inv_k * gk_ref[:, cols]).astype(BF)
        s1 = lax.dot_general(q, k, contract, preferred_element_type=F32) * SCALE
        s2 = lax.dot_general(q, part(2), contract, preferred_element_type=F32) * SCALE
        s2 = jnp.where(live, s2, NEGATIVE)
        peak = jnp.max(jnp.maximum(s1, s2), axis=1, keepdims=True).astype(BF).astype(F32)
        w1 = jnp.exp(s1 - peak)
        w2 = jnp.where(live, jnp.exp(s2 - peak), 0.0)
        total = jnp.sum(w1 + w2, axis=1, keepdims=True)
        mixed = jnp.dot(w1.astype(BF), part(1), preferred_element_type=F32) + jnp.dot(
            w2.astype(BF), part(3), preferred_element_type=F32
        )
        out_ref[:, :, cols] = (mixed / total).astype(BF).reshape(QB, ROWS, HEAD_DIM)
        high = total.astype(BF).astype(F32)
        stats = jnp.where(lane == h, peak, stats)
        stats = jnp.where(lane == HEADS + h, high, stats)
        stats = jnp.where(lane == 2 * HEADS + h, total - high, stats)
    out_ref[:, :, FEAT:] = stats.astype(BF).reshape(QB, ROWS, 128)


def project_kernel(part_ref, weight_ref, out_ref):
    stats = [part_ref[j, :, FEAT:].astype(F32) for j in range(QB)]
    pieces = []
    for h in range(HEADS):
        peaks = [s[:, h : h + 1] for s in stats]
        totals = [
            s[:, HEADS + h : HEADS + h + 1] + s[:, 2 * HEADS + h : 2 * HEADS + h + 1] for s in stats
        ]
        peak = peaks[0]
        for other in peaks[1:]:
            peak = jnp.maximum(peak, other)
        shares = [t * jnp.exp(m - peak) for t, m in zip(totals, peaks)]
        total = sum(shares)
        cols = slice(h * HEAD_DIM, (h + 1) * HEAD_DIM)
        mixed = sum(part_ref[j, :, cols].astype(F32) * shares[j] for j in range(QB))
        pieces.append((mixed / total).astype(BF))
    attended = jnp.concatenate(pieces, axis=1)
    for w in range(HB):
        out_ref[w] = jnp.dot(
            attended, weight_ref[:, w * WIDTH : (w + 1) * WIDTH], preferred_element_type=F32
        ).astype(BF)


def finish_kernel(step_ref, part_ref, hidden_ref, gate_ref, out_ref):
    projected = part_ref[0].astype(F32)
    for h in range(1, HB):
        projected = projected + part_ref[h].astype(F32)
    gate = gate_ref[pl.ds(step_ref[0], 1), :]
    out_ref[...] = (hidden_ref[...].astype(F32) + gate * projected).astype(BF)


def to_all(block, axes, count):
    spread = jnp.broadcast_to(block[None], (count,) + block.shape)
    return lax.all_to_all(spread, axes, 0, 0, tiled=True)


def shards(
    hidden,
    query,
    key,
    value,
    query_gain,
    key_gain,
    ref_key,
    ref_value,
    ref_count,
    out_weight,
    gate_table,
    frame_step,
):
    counts = jnp.broadcast_to(ref_count.astype(BF)[:, None], (ROWS, 128))
    block = jnp.concatenate([key, value, ref_key, ref_value, counts], axis=1)
    kv = lax.all_gather(block, KEY_AXES, axis=0)
    queries = to_all(query, QUERY_AXES, QB)
    powers = call(power_kernel, jax.ShapeDtypeStruct((HB, 8, 128), F32), queries, kv)
    powers = lax.all_to_all(powers, HEAD_AXES, 0, 0, tiled=True)
    parts = call(
        attend_kernel,
        jax.ShapeDtypeStruct((QB, ROWS, FEAT + 128), BF),
        queries,
        kv,
        powers,
        query_gain[None],
        key_gain[None],
    )
    parts = lax.all_to_all(parts, QUERY_AXES, 0, 0, tiled=True)
    projected = call(
        project_kernel, jax.ShapeDtypeStruct((HB, ROWS, WIDTH), BF), parts, out_weight
    )
    projected = lax.all_to_all(projected, HEAD_AXES, 0, 0, tiled=True)
    vmem = pl.BlockSpec(memory_space=pltpu.VMEM)
    return call(
        finish_kernel,
        jax.ShapeDtypeStruct((ROWS, WIDTH), BF),
        frame_step,
        projected,
        hidden,
        gate_table,
        in_specs=[pl.BlockSpec(memory_space=pltpu.SMEM), vmem, vmem, vmem],
    )


def solution(mesh):
    wide = Mesh(mesh.devices.reshape(2, 4, 8, 4, 2), HEAD_AXES + SEQ_AXES)
    both = P(SEQ_AXES, HEAD_AXES)
    in_specs = (
        both,
        both,
        both,
        both,
        P(HEAD_AXES),
        P(HEAD_AXES),
        both,
        both,
        P(SEQ_AXES),
        P(HEAD_AXES, None),
        P(None, HEAD_AXES),
        P(SEQ_AXES),
    )
    return jax.shard_map(shards, mesh=wide, in_specs=in_specs, out_specs=both, check_vma=False)
```

```python
import math

import jax
import jax.numpy as jnp
from jax import lax
from jax.experimental import pallas as pl
from jax.experimental.pallas import tpu as pltpu
from jax.sharding import Mesh
from jax.sharding import PartitionSpec as P

HEAD_DIM = 128
HEADS = 3
FEAT = HEADS * HEAD_DIM
ROWS = 32
WIDTH = 640
ALL_FEATURES = 3072
EPSILON = 1e-06
NEGATIVE = -1e30
SCALE = 1.0 / math.sqrt(HEAD_DIM)
BF = jnp.bfloat16
F32 = jnp.float32

HEAD_AXES = ("yl", "x")
SEQ_AXES = ("z", "yh", "c")
KEY_AXES = ("yh", "c")
QUERY_AXES = "z"
QB = 8
KB = 8
HB = 8


def call(kernel, out_shape, *args, in_specs=None, n_out=1, cost=1, mib=16, scratch=()):
    vmem = pl.BlockSpec(memory_space=pltpu.VMEM)
    return pl.pallas_call(
        kernel,
        out_shape=out_shape,
        in_specs=in_specs or [vmem] * len(args),
        out_specs=vmem if n_out == 1 else [vmem] * n_out,
        scratch_shapes=scratch,
        cost_estimate=pl.CostEstimate(flops=cost, bytes_accessed=cost, transcendentals=0),
        compiler_params=pltpu.CompilerParams(vmem_limit_bytes=mib * 1024 * 1024),
    )(*args)


def pack_kernel(count_ref, q_ref, k_ref, v_ref, rk_ref, rv_ref, qb_ref, kv_ref):
    query = q_ref[...]
    for peer in range(QB):
        qb_ref[peer] = query
    for t, ref in enumerate((k_ref, v_ref, rk_ref, rv_ref)):
        kv_ref[:, t * FEAT : (t + 1) * FEAT] = ref[...]
    count = count_ref[0].astype(F32)
    kv_ref[:, 4 * FEAT :] = jnp.full((ROWS, 128), count, F32).astype(BF)


def token_power(rows):
    wide = rows.astype(F32)
    squares = wide * wide
    part = squares[:, :128] + squares[:, 128:256] + squares[:, 256:]
    return jnp.sum(part.T, axis=0, keepdims=True)


def power_kernel(q_ref, kv_ref, out_ref):
    lines = []
    for g in range(2):
        lines.append(token_power(q_ref[g * 4 : g * 4 + 4].reshape(128, FEAT)))
    for g in range(2):
        lines.append(token_power(kv_ref[g * 4 : g * 4 + 4, :, :FEAT].reshape(128, FEAT)))
    block = jnp.concatenate(lines + [jnp.zeros((4, 128), F32)], axis=0)
    for peer in range(HB):
        out_ref[peer] = block


def attend_kernel(q_ref, kv_ref, pw_ref, gq_ref, gk_ref, out_ref):
    power = jnp.sum(pw_ref[...], axis=0) / ALL_FEATURES
    inverse = lax.rsqrt(power + EPSILON)

    def columns(first):
        tiles = [
            jnp.broadcast_to(inverse[first + g : first + g + 1], (128, 128)).T for g in range(2)
        ]
        return jnp.concatenate(tiles, axis=0)

    inv_q = columns(0)
    inv_k = columns(2)
    n_keys = KB * ROWS
    slot = lax.broadcasted_iota(jnp.int32, (1, n_keys), 1)
    counts = jnp.zeros((1, n_keys), F32)
    for p in range(KB):
        line = kv_ref[p, 0:16, 4 * FEAT :][0:1].astype(F32)
        counts = jnp.where(slot // ROWS == p, jnp.concatenate([line, line], axis=1), counts)
    live = (slot % ROWS).astype(F32) < counts
    lane = lax.broadcasted_iota(jnp.int32, (QB * ROWS, 128), 1)
    stats = jnp.zeros((QB * ROWS, 128), F32)
    contract = (((1,), (1,)), ((), ()))
    for h in range(HEADS):
        cols = slice(h * HEAD_DIM, (h + 1) * HEAD_DIM)

        def part(t):
            return kv_ref[:, :, t * FEAT + h * HEAD_DIM : t * FEAT + (h + 1) * HEAD_DIM].reshape(
                n_keys, HEAD_DIM
            )

        q = q_ref[:, :, cols].reshape(QB * ROWS, HEAD_DIM).astype(F32)
        q = (q * inv_q * gq_ref[:, cols]).astype(BF)
        k = (part(0).astype(F32) * inv_k * gk_ref[:, cols]).astype(BF)
        s1 = lax.dot_general(q, k, contract, preferred_element_type=F32) * SCALE
        s2 = lax.dot_general(q, part(2), contract, preferred_element_type=F32) * SCALE
        s2 = jnp.where(live, s2, NEGATIVE)
        peak = jnp.max(jnp.maximum(s1, s2), axis=1, keepdims=True).astype(BF).astype(F32)
        w1 = jnp.exp(s1 - peak)
        w2 = jnp.where(live, jnp.exp(s2 - peak), 0.0)
        total = jnp.sum(w1 + w2, axis=1, keepdims=True)
        mixed = jnp.dot(w1.astype(BF), part(1), preferred_element_type=F32) + jnp.dot(
            w2.astype(BF), part(3), preferred_element_type=F32
        )
        out_ref[:, :, cols] = (mixed / total).astype(BF).reshape(QB, ROWS, HEAD_DIM)
        high = total.astype(BF).astype(F32)
        stats = jnp.where(lane == h, peak, stats)
        stats = jnp.where(lane == HEADS + h, high, stats)
        stats = jnp.where(lane == 2 * HEADS + h, total - high, stats)
    out_ref[:, :, FEAT:] = stats.astype(BF).reshape(QB, ROWS, 128)


def project_kernel(part_ref, weight_hbm, out_ref, weight_ref, sems):
    copies = [
        pltpu.make_async_copy(
            weight_hbm.at[:, w * WIDTH : (w + 1) * WIDTH],
            weight_ref.at[:, w * WIDTH : (w + 1) * WIDTH],
            sems.at[w],
        )
        for w in range(HB)
    ]
    for copy in copies:
        copy.start()
    stats = [part_ref[j, :, FEAT:].astype(F32) for j in range(QB)]
    pieces = []
    for h in range(HEADS):
        peaks = [s[:, h : h + 1] for s in stats]
        totals = [
            s[:, HEADS + h : HEADS + h + 1] + s[:, 2 * HEADS + h : 2 * HEADS + h + 1] for s in stats
        ]
        peak = peaks[0]
        for other in peaks[1:]:
            peak = jnp.maximum(peak, other)
        shares = [t * jnp.exp(m - peak) for t, m in zip(totals, peaks)]
        total = sum(shares)
        cols = slice(h * HEAD_DIM, (h + 1) * HEAD_DIM)
        mixed = sum(part_ref[j, :, cols].astype(F32) * shares[j] for j in range(QB))
        pieces.append((mixed / total).astype(BF))
    attended = jnp.concatenate(pieces, axis=1)
    for w in range(HB):
        copies[w].wait()
        out_ref[w] = jnp.dot(
            attended, weight_ref[:, w * WIDTH : (w + 1) * WIDTH], preferred_element_type=F32
        ).astype(BF)


def finish_kernel(step_ref, part_ref, hidden_ref, gate_ref, out_ref):
    projected = part_ref[0].astype(F32)
    for h in range(1, HB):
        projected = projected + part_ref[h].astype(F32)
    gate = gate_ref[pl.ds(step_ref[0], 1), :]
    out_ref[...] = (hidden_ref[...].astype(F32) + gate * projected).astype(BF)


def shards(
    hidden,
    query,
    key,
    value,
    query_gain,
    key_gain,
    ref_key,
    ref_value,
    ref_count,
    out_weight,
    gate_table,
    frame_step,
):
    vmem = pl.BlockSpec(memory_space=pltpu.VMEM)
    queries, block = call(
        pack_kernel,
        (
            jax.ShapeDtypeStruct((QB, ROWS, FEAT), BF),
            jax.ShapeDtypeStruct((ROWS, 4 * FEAT + 128), BF),
        ),
        ref_count,
        query,
        key,
        value,
        ref_key,
        ref_value,
        in_specs=[pl.BlockSpec(memory_space=pltpu.SMEM)] + [vmem] * 5,
        n_out=2,
        mib=60,
    )
    queries = lax.all_to_all(queries, QUERY_AXES, 0, 0, tiled=True)
    kv = lax.all_gather(block, "yh", axis=0)
    kv = lax.all_gather(kv, "c", axis=0, tiled=True)
    powers = call(power_kernel, jax.ShapeDtypeStruct((HB, 8, 128), F32), queries, kv)
    powers = lax.all_to_all(powers, HEAD_AXES, 0, 0, tiled=True)
    parts = call(
        attend_kernel,
        jax.ShapeDtypeStruct((QB, ROWS, FEAT + 128), BF),
        queries,
        kv,
        powers,
        query_gain[None],
        key_gain[None],
        cost=4 * 1024 * 1024,
    )
    parts = lax.all_to_all(parts, QUERY_AXES, 0, 0, tiled=True)
    projected = call(
        project_kernel,
        jax.ShapeDtypeStruct((HB, ROWS, WIDTH), BF),
        parts,
        out_weight,
        in_specs=[vmem, pl.BlockSpec(memory_space=pl.ANY)],
        cost=6 * 1024 * 1024,
        mib=60,
        scratch=[pltpu.VMEM(out_weight.shape, BF), pltpu.SemaphoreType.DMA((HB,))],
    )
    projected = lax.all_to_all(projected, HEAD_AXES, 0, 0, tiled=True)
    return call(
        finish_kernel,
        jax.ShapeDtypeStruct((ROWS, WIDTH), BF),
        frame_step,
        projected,
        hidden,
        gate_table,
        in_specs=[pl.BlockSpec(memory_space=pltpu.SMEM), vmem, vmem, vmem],
    )


def solution(mesh):
    wide = Mesh(mesh.devices.reshape(2, 4, 8, 4, 2), HEAD_AXES + SEQ_AXES)
    both = P(SEQ_AXES, HEAD_AXES)
    in_specs = (
        both,
        both,
        both,
        both,
        P(HEAD_AXES),
        P(HEAD_AXES),
        both,
        both,
        P(SEQ_AXES),
        P(HEAD_AXES, None),
        P(None, HEAD_AXES),
        P(SEQ_AXES),
    )
    return jax.shard_map(shards, mesh=wide, in_specs=in_specs, out_specs=both, check_vma=False)
```

```python
import math

import jax
import jax.numpy as jnp
from jax import lax
from jax.experimental import pallas as pl
from jax.experimental.pallas import tpu as pltpu
from jax.sharding import Mesh
from jax.sharding import PartitionSpec as P

HEAD_DIM = 128
HEADS = 3
FEAT = HEADS * HEAD_DIM
ROWS = 32
STATS = 16
PIECE = HEADS * ROWS + STATS
WIDTH = 640
ALL_FEATURES = 3072
EPSILON = 1e-06
NEGATIVE = -1e30
SCALE = 1.0 / math.sqrt(HEAD_DIM)
BF = jnp.bfloat16
F32 = jnp.float32

HEAD_AXES = ("yl", "x")
SEQ_AXES = ("z", "yh", "c")
KEY_AXES = ("yh", "c")
QUERY_AXES = "z"
QB = 8
KB = 8
HB = 8


def call(kernel, out_shape, *args, in_specs=None, n_out=1, cost=1, mib=16, scratch=()):
    vmem = pl.BlockSpec(memory_space=pltpu.VMEM)
    return pl.pallas_call(
        kernel,
        out_shape=out_shape,
        in_specs=in_specs or [vmem] * len(args),
        out_specs=vmem if n_out == 1 else [vmem] * n_out,
        scratch_shapes=scratch,
        cost_estimate=pl.CostEstimate(flops=cost, bytes_accessed=cost, transcendentals=0),
        compiler_params=pltpu.CompilerParams(vmem_limit_bytes=mib * 1024 * 1024),
    )(*args)


def pack_kernel(count_ref, q_ref, k_ref, v_ref, rk_ref, rv_ref, qb_ref, kv_ref):
    query = q_ref[...]
    for peer in range(QB):
        qb_ref[peer] = query
    for t, ref in enumerate((k_ref, v_ref, rk_ref, rv_ref)):
        kv_ref[:, t * FEAT : (t + 1) * FEAT] = ref[...]
    count = count_ref[0].astype(F32)
    kv_ref[:, 4 * FEAT :] = jnp.full((ROWS, 128), count, F32).astype(BF)


def token_power(rows):
    wide = rows.astype(F32)
    squares = wide * wide
    part = squares[:, :128] + squares[:, 128:256] + squares[:, 256:]
    return jnp.sum(part.T, axis=0, keepdims=True)


def power_kernel(q_ref, kv_ref, out_ref):
    lines = []
    for g in range(2):
        lines.append(token_power(q_ref[g * 4 : g * 4 + 4].reshape(128, FEAT)))
    for g in range(2):
        lines.append(token_power(kv_ref[g * 4 : g * 4 + 4, :, :FEAT].reshape(128, FEAT)))
    block = jnp.concatenate(lines + [jnp.zeros((4, 128), F32)], axis=0)
    for peer in range(HB):
        out_ref[peer] = block


def attend_kernel(q_ref, kv_ref, pw_ref, gq_ref, gk_ref, weight_ref, out_ref):
    power = jnp.sum(pw_ref[...], axis=0) / ALL_FEATURES
    inverse = lax.rsqrt(power + EPSILON)

    def columns(first):
        tiles = [
            jnp.broadcast_to(inverse[first + g : first + g + 1], (128, 128)).T for g in range(2)
        ]
        return jnp.concatenate(tiles, axis=0)

    inv_q = columns(0)
    inv_k = columns(2)
    n_keys = KB * ROWS
    slot = lax.broadcasted_iota(jnp.int32, (1, n_keys), 1)
    counts = jnp.zeros((1, n_keys), F32)
    for p in range(KB):
        line = kv_ref[p, 0:16, 4 * FEAT :][0:1].astype(F32)
        counts = jnp.where(slot // ROWS == p, jnp.concatenate([line, line], axis=1), counts)
    live = (slot % ROWS).astype(F32) < counts
    lane = lax.broadcasted_iota(jnp.int32, (QB * ROWS, 128), 1)
    stats = jnp.zeros((QB * ROWS, 128), F32)
    contract = (((1,), (1,)), ((), ()))
    for h in range(HEADS):
        cols = slice(h * HEAD_DIM, (h + 1) * HEAD_DIM)

        def part(t):
            return kv_ref[:, :, t * FEAT + h * HEAD_DIM : t * FEAT + (h + 1) * HEAD_DIM].reshape(
                n_keys, HEAD_DIM
            )

        q = q_ref[:, :, cols].reshape(QB * ROWS, HEAD_DIM).astype(F32)
        q = (q * inv_q * gq_ref[:, cols]).astype(BF)
        k = (part(0).astype(F32) * inv_k * gk_ref[:, cols]).astype(BF)
        s1 = lax.dot_general(q, k, contract, preferred_element_type=F32) * SCALE
        s2 = lax.dot_general(q, part(2), contract, preferred_element_type=F32) * SCALE
        s2 = jnp.where(live, s2, NEGATIVE)
        peak = jnp.max(jnp.maximum(s1, s2), axis=1, keepdims=True).astype(BF).astype(F32)
        w1 = jnp.exp(s1 - peak)
        w2 = jnp.where(live, jnp.exp(s2 - peak), 0.0)
        total = jnp.sum(w1 + w2, axis=1, keepdims=True)
        mixed = jnp.dot(w1.astype(BF), part(1), preferred_element_type=F32) + jnp.dot(
            w2.astype(BF), part(3), preferred_element_type=F32
        )
        out_ref[:, h * ROWS : (h + 1) * ROWS] = (
            (mixed / total).astype(BF).reshape(QB, ROWS, HEAD_DIM)
        )
        high = total.astype(BF).astype(F32)
        stats = jnp.where(lane == h, peak, stats)
        stats = jnp.where(lane == HEADS + h, high, stats)
        stats = jnp.where(lane == 2 * HEADS + h, total - high, stats)
    for half in range(2):
        lines = stats[half * 128 : (half + 1) * 128].T[:STATS]
        for j in range(4):
            turned = lines if j == 0 else pltpu.roll(lines, 128 - j * ROWS, 1)
            out_ref[half * 4 + j, HEADS * ROWS :] = turned.astype(BF)


def project_kernel(part_ref, weight_ref, out_ref):
    stats = part_ref[:, HEADS * ROWS :].astype(F32).reshape(QB * STATS, 128).T[:ROWS]
    pieces = []
    for h in range(HEADS):

        def column(j, s):
            return stats[:, j * STATS + s * HEADS + h : j * STATS + s * HEADS + h + 1]

        peaks = [column(j, 0) for j in range(QB)]
        totals = [column(j, 1) + column(j, 2) for j in range(QB)]
        peak = peaks[0]
        for other in peaks[1:]:
            peak = jnp.maximum(peak, other)
        shares = [t * jnp.exp(m - peak) for t, m in zip(totals, peaks)]
        total = sum(shares)
        mixed = sum(
            part_ref[j, h * ROWS : (h + 1) * ROWS].astype(F32) * shares[j] for j in range(QB)
        )
        pieces.append((mixed / total).astype(BF))
    attended = jnp.concatenate(pieces, axis=1)
    for w in range(HB):
        out_ref[w] = jnp.dot(
            attended, weight_ref[:, w * WIDTH : (w + 1) * WIDTH], preferred_element_type=F32
        ).astype(BF)


def finish_kernel(step_ref, part_ref, hidden_ref, gate_ref, out_ref):
    projected = part_ref[0].astype(F32)
    for h in range(1, HB):
        projected = projected + part_ref[h].astype(F32)
    gate = gate_ref[pl.ds(step_ref[0], 1), :]
    out_ref[...] = (hidden_ref[...].astype(F32) + gate * projected).astype(BF)


def shards(
    hidden,
    query,
    key,
    value,
    query_gain,
    key_gain,
    ref_key,
    ref_value,
    ref_count,
    out_weight,
    gate_table,
    frame_step,
):
    vmem = pl.BlockSpec(memory_space=pltpu.VMEM)
    queries, block = call(
        pack_kernel,
        (
            jax.ShapeDtypeStruct((QB, ROWS, FEAT), BF),
            jax.ShapeDtypeStruct((ROWS, 4 * FEAT + 128), BF),
        ),
        ref_count,
        query,
        key,
        value,
        ref_key,
        ref_value,
        in_specs=[pl.BlockSpec(memory_space=pltpu.SMEM)] + [vmem] * 5,
        n_out=2,
        mib=60,
    )
    queries = lax.all_to_all(queries, QUERY_AXES, 0, 0, tiled=True)
    kv = lax.all_gather(block, KEY_AXES, axis=0)
    powers = call(power_kernel, jax.ShapeDtypeStruct((HB, 8, 128), F32), queries, kv)
    powers = lax.all_to_all(powers, HEAD_AXES, 0, 0, tiled=True)
    parts = call(
        attend_kernel,
        jax.ShapeDtypeStruct((QB, PIECE, HEAD_DIM), BF),
        queries,
        kv,
        powers,
        query_gain[None],
        key_gain[None],
        out_weight,
        in_specs=[vmem] * 5 + [pl.BlockSpec(memory_space=pl.ANY)],
        mib=50,
        cost=4 * 1024 * 1024,
    )
    parts = lax.all_to_all(parts, QUERY_AXES, 0, 0, tiled=True)
    projected = call(
        project_kernel,
        jax.ShapeDtypeStruct((HB, ROWS, WIDTH), BF),
        parts,
        out_weight,
        cost=6 * 1024 * 1024,
    )
    projected = lax.all_to_all(projected, HEAD_AXES, 0, 0, tiled=True)
    return call(
        finish_kernel,
        jax.ShapeDtypeStruct((ROWS, WIDTH), BF),
        frame_step,
        projected,
        hidden,
        gate_table,
        in_specs=[pl.BlockSpec(memory_space=pltpu.SMEM), vmem, vmem, vmem],
    )


def solution(mesh):
    wide = Mesh(mesh.devices.reshape(2, 4, 8, 4, 2), HEAD_AXES + SEQ_AXES)
    both = P(SEQ_AXES, HEAD_AXES)
    in_specs = (
        both,
        both,
        both,
        both,
        P(HEAD_AXES),
        P(HEAD_AXES),
        both,
        both,
        P(SEQ_AXES),
        P(HEAD_AXES, None),
        P(None, HEAD_AXES),
        P(SEQ_AXES),
    )
    return jax.shard_map(shards, mesh=wide, in_specs=in_specs, out_specs=both, check_vma=False)
```

```python
import math

import jax
import jax.numpy as jnp
from jax import lax
from jax.experimental import pallas as pl
from jax.experimental.pallas import tpu as pltpu
from jax.sharding import Mesh
from jax.sharding import PartitionSpec as P

HEAD_DIM = 128
HEADS = 3
FEAT = HEADS * HEAD_DIM
ROWS = 32
STATS = 16
PIECE = HEADS * ROWS + STATS
WIDTH = 640
ALL_FEATURES = 3072
EPSILON = 1e-06
NEGATIVE = -1e30
SCALE = 1.0 / math.sqrt(HEAD_DIM)
BF = jnp.bfloat16
F32 = jnp.float32

HEAD_AXES = ("yl", "x")
SEQ_AXES = ("z", "yh", "c")
KEY_AXES = ("yh", "c")
QUERY_AXES = "z"
QB = 8
KB = 8
HB = 8


def call(kernel, out_shape, *args, in_specs=None, n_out=1, cost=1, mib=16, scratch=()):
    vmem = pl.BlockSpec(memory_space=pltpu.VMEM)
    return pl.pallas_call(
        kernel,
        out_shape=out_shape,
        in_specs=in_specs or [vmem] * len(args),
        out_specs=vmem if n_out == 1 else [vmem] * n_out,
        scratch_shapes=scratch,
        cost_estimate=pl.CostEstimate(flops=cost, bytes_accessed=cost, transcendentals=0),
        compiler_params=pltpu.CompilerParams(vmem_limit_bytes=mib * 1024 * 1024),
    )(*args)


def power_kernel(q_ref, k_ref, out_ref):
    rows = jnp.concatenate([q_ref[...], k_ref[...], q_ref[...], k_ref[...]], axis=0)
    wide = rows.astype(F32)
    squares = wide * wide
    part = squares[:, :128] + squares[:, 128:256] + squares[:, 256:]
    block = jnp.broadcast_to(jnp.sum(part.T, axis=0, keepdims=True), (8, 128))
    for peer in range(HB):
        out_ref[peer] = block


def stage_kernel(count_ref, q_ref, k_ref, v_ref, rk_ref, rv_ref, out_ref):
    for t, ref in enumerate((q_ref, k_ref, v_ref, rk_ref, rv_ref)):
        out_ref[:, t * FEAT : (t + 1) * FEAT] = ref[...]
    count = count_ref[0].astype(F32)
    out_ref[:, 5 * FEAT :] = jnp.full((ROWS, 128), count, F32).astype(BF)


def pack_kernel(pw_ref, gq_ref, gk_ref, staged_ref, qb_ref, kv_ref):
    power = jnp.sum(pw_ref[...], axis=0)[0:1] / ALL_FEATURES
    inverse = jnp.broadcast_to(lax.rsqrt(power + EPSILON), (128, 128)).T
    inverse = jnp.concatenate([inverse] * HEADS, axis=1)
    query = staged_ref[:, :FEAT].astype(F32)
    query = (query * inverse[:ROWS] * gq_ref[...]).astype(BF)
    for peer in range(QB):
        qb_ref[peer] = query
    key = staged_ref[:, FEAT : 2 * FEAT].astype(F32)
    kv_ref[:, :FEAT] = (key * inverse[ROWS : 2 * ROWS] * gk_ref[...]).astype(BF)
    kv_ref[:, FEAT:] = staged_ref[:, 2 * FEAT :]


def attend_kernel(q_ref, kv_ref, weight_ref, out_ref):
    n_keys = KB * ROWS
    slot = lax.broadcasted_iota(jnp.int32, (1, n_keys), 1)
    counts = jnp.zeros((1, n_keys), F32)
    for p in range(KB):
        line = kv_ref[p, 0:16, 4 * FEAT :][0:1].astype(F32)
        counts = jnp.where(slot // ROWS == p, jnp.concatenate([line, line], axis=1), counts)
    live = (slot % ROWS).astype(F32) < counts
    lane = lax.broadcasted_iota(jnp.int32, (QB * ROWS, 128), 1)
    stats = jnp.zeros((QB * ROWS, 128), F32)
    contract = (((1,), (1,)), ((), ()))
    for h in range(HEADS):
        cols = slice(h * HEAD_DIM, (h + 1) * HEAD_DIM)

        def part(t):
            return kv_ref[:, :, t * FEAT + h * HEAD_DIM : t * FEAT + (h + 1) * HEAD_DIM].reshape(
                n_keys, HEAD_DIM
            )

        q = q_ref[:, :, cols].reshape(QB * ROWS, HEAD_DIM)
        s1 = lax.dot_general(q, part(0), contract, preferred_element_type=F32) * SCALE
        s2 = lax.dot_general(q, part(2), contract, preferred_element_type=F32) * SCALE
        s2 = jnp.where(live, s2, NEGATIVE)
        peak = jnp.max(jnp.maximum(s1, s2), axis=1, keepdims=True).astype(BF).astype(F32)
        w1 = jnp.exp(s1 - peak)
        w2 = jnp.where(live, jnp.exp(s2 - peak), 0.0)
        total = jnp.sum(w1 + w2, axis=1, keepdims=True)
        mixed = jnp.dot(w1.astype(BF), part(1), preferred_element_type=F32) + jnp.dot(
            w2.astype(BF), part(3), preferred_element_type=F32
        )
        out_ref[:, h * ROWS : (h + 1) * ROWS] = (
            (mixed / total).astype(BF).reshape(QB, ROWS, HEAD_DIM)
        )
        high = total.astype(BF).astype(F32)
        stats = jnp.where(lane == h, peak, stats)
        stats = jnp.where(lane == HEADS + h, high, stats)
        stats = jnp.where(lane == 2 * HEADS + h, total - high, stats)
    for half in range(2):
        lines = stats[half * 128 : (half + 1) * 128].T[:STATS]
        for j in range(4):
            turned = lines if j == 0 else pltpu.roll(lines, 128 - j * ROWS, 1)
            out_ref[half * 4 + j, HEADS * ROWS :] = turned.astype(BF)


def project_kernel(part_ref, weight_ref, out_ref):
    stats = part_ref[:, HEADS * ROWS :].astype(F32).reshape(QB * STATS, 128).T[:ROWS]
    pieces = []
    for h in range(HEADS):

        def column(j, s):
            return stats[:, j * STATS + s * HEADS + h : j * STATS + s * HEADS + h + 1]

        peaks = [column(j, 0) for j in range(QB)]
        totals = [column(j, 1) + column(j, 2) for j in range(QB)]
        peak = peaks[0]
        for other in peaks[1:]:
            peak = jnp.maximum(peak, other)
        shares = [t * jnp.exp(m - peak) for t, m in zip(totals, peaks)]
        total = sum(shares)
        mixed = sum(
            part_ref[j, h * ROWS : (h + 1) * ROWS].astype(F32) * shares[j] for j in range(QB)
        )
        pieces.append((mixed / total).astype(BF))
    attended = jnp.concatenate(pieces, axis=1)
    for w in range(HB):
        out_ref[w] = jnp.dot(
            attended, weight_ref[:, w * WIDTH : (w + 1) * WIDTH], preferred_element_type=F32
        ).astype(BF)


def finish_kernel(step_ref, part_ref, hidden_ref, gate_ref, out_ref):
    projected = part_ref[0].astype(F32)
    for h in range(1, HB):
        projected = projected + part_ref[h].astype(F32)
    gate = gate_ref[pl.ds(step_ref[0], 1), :]
    out_ref[...] = (hidden_ref[...].astype(F32) + gate * projected).astype(BF)


def shards(
    hidden,
    query,
    key,
    value,
    query_gain,
    key_gain,
    ref_key,
    ref_value,
    ref_count,
    out_weight,
    gate_table,
    frame_step,
):
    vmem = pl.BlockSpec(memory_space=pltpu.VMEM)
    powers = call(
        power_kernel, jax.ShapeDtypeStruct((HB, 8, 128), F32), query, key, mib=60
    )
    powers = lax.all_to_all(powers, HEAD_AXES, 0, 0, tiled=True)
    staged = call(
        stage_kernel,
        jax.ShapeDtypeStruct((ROWS, 5 * FEAT + 128), BF),
        ref_count,
        query,
        key,
        value,
        ref_key,
        ref_value,
        in_specs=[pl.BlockSpec(memory_space=pltpu.SMEM)] + [vmem] * 5,
        mib=52,
    )
    queries, block = call(
        pack_kernel,
        (
            jax.ShapeDtypeStruct((QB, ROWS, FEAT), BF),
            jax.ShapeDtypeStruct((ROWS, 4 * FEAT + 128), BF),
        ),
        powers,
        query_gain[None],
        key_gain[None],
        staged,
        n_out=2,
    )
    queries = lax.all_to_all(queries, QUERY_AXES, 0, 0, tiled=True)
    kv = lax.all_gather(block, KEY_AXES, axis=0)
    parts = call(
        attend_kernel,
        jax.ShapeDtypeStruct((QB, PIECE, HEAD_DIM), BF),
        queries,
        kv,
        out_weight,
        in_specs=[vmem] * 2 + [pl.BlockSpec(memory_space=pl.ANY)],
        mib=50,
        cost=4 * 1024 * 1024,
    )
    parts = lax.all_to_all(parts, QUERY_AXES, 0, 0, tiled=True)
    projected = call(
        project_kernel,
        jax.ShapeDtypeStruct((HB, ROWS, WIDTH), BF),
        parts,
        out_weight,
        cost=6 * 1024 * 1024,
    )
    projected = lax.all_to_all(projected, HEAD_AXES, 0, 0, tiled=True)
    return call(
        finish_kernel,
        jax.ShapeDtypeStruct((ROWS, WIDTH), BF),
        frame_step,
        projected,
        hidden,
        gate_table,
        in_specs=[pl.BlockSpec(memory_space=pltpu.SMEM), vmem, vmem, vmem],
    )


def solution(mesh):
    wide = Mesh(mesh.devices.reshape(2, 4, 8, 4, 2), HEAD_AXES + SEQ_AXES)
    both = P(SEQ_AXES, HEAD_AXES)
    in_specs = (
        both,
        both,
        both,
        both,
        P(HEAD_AXES),
        P(HEAD_AXES),
        both,
        both,
        P(SEQ_AXES),
        P(HEAD_AXES, None),
        P(None, HEAD_AXES),
        P(SEQ_AXES),
    )
    return jax.shard_map(shards, mesh=wide, in_specs=in_specs, out_specs=both, check_vma=False)
```

```python
import math

import jax
import jax.numpy as jnp
from jax import lax
from jax.experimental import pallas as pl
from jax.experimental.pallas import tpu as pltpu
from jax.sharding import Mesh
from jax.sharding import PartitionSpec as P

HEAD_DIM = 128
HEADS = 3
FEAT = HEADS * HEAD_DIM
ROWS = 32
STATS = 16
PIECE = HEADS * ROWS + STATS
WIDTH = 640
ALL_FEATURES = 3072
EPSILON = 1e-06
NEGATIVE = -1e30
SCALE = 1.0 / math.sqrt(HEAD_DIM)
BF = jnp.bfloat16
F32 = jnp.float32

HEAD_AXES = ("yl", "x")
SEQ_AXES = ("z", "yh", "c")
KEY_AXES = ("yh", "c")
QUERY_AXES = "z"
QB = 8
KB = 8
HB = 8


def call(kernel, out_shape, *args, in_specs=None, n_out=1, cost=1, mib=16, scratch=()):
    vmem = pl.BlockSpec(memory_space=pltpu.VMEM)
    return pl.pallas_call(
        kernel,
        out_shape=out_shape,
        in_specs=in_specs or [vmem] * len(args),
        out_specs=vmem if n_out == 1 else [vmem] * n_out,
        scratch_shapes=scratch,
        cost_estimate=pl.CostEstimate(flops=cost, bytes_accessed=cost, transcendentals=0),
        compiler_params=pltpu.CompilerParams(vmem_limit_bytes=mib * 1024 * 1024),
    )(*args)


def pack_kernel(
    count_ref, gq_ref, gk_ref, q_ref, k_ref, v_ref, rk_ref, rv_ref, qb_ref, kv_ref
):
    query = q_ref[...]
    for peer in range(QB):
        qb_ref[peer] = query
    for t, ref in enumerate((k_ref, v_ref, rk_ref, rv_ref)):
        kv_ref[:, t * FEAT : (t + 1) * FEAT] = ref[...]
    count = count_ref[0].astype(F32)
    parts = []
    for ref in (gq_ref, gk_ref):
        rest = ref[...]
        for _ in range(3):
            part = rest.astype(BF).astype(F32)
            parts += [part[h * 128 : (h + 1) * 128].reshape(1, 128) for h in range(HEADS)]
            rest = rest - part
    lines = [jnp.full((1, 128), count, F32)] + parts + [jnp.zeros((ROWS - 19, 128), F32)]
    kv_ref[:, 4 * FEAT :] = jnp.concatenate(lines, axis=0).astype(BF)


def token_power(rows):
    wide = rows.astype(F32)
    squares = wide * wide
    part = squares[:, :128] + squares[:, 128:256] + squares[:, 256:]
    return jnp.sum(part.T, axis=0, keepdims=True)


def power_kernel(q_ref, kv_ref, out_ref):
    lines = []
    for g in range(2):
        lines.append(token_power(q_ref[g * 4 : g * 4 + 4].reshape(128, FEAT)))
    for g in range(2):
        lines.append(token_power(kv_ref[g * 4 : g * 4 + 4, :, :FEAT].reshape(128, FEAT)))
    block = jnp.concatenate(lines + [jnp.zeros((4, 128), F32)], axis=0)
    for peer in range(HB):
        out_ref[peer] = block


def attend_kernel(q_ref, kv_ref, pw_ref, weight_ref, out_ref):
    power = jnp.sum(pw_ref[...], axis=0) / ALL_FEATURES
    inverse = lax.rsqrt(power + EPSILON)

    def columns(first):
        tiles = [
            jnp.broadcast_to(inverse[first + g : first + g + 1], (128, 128)).T for g in range(2)
        ]
        return jnp.concatenate(tiles, axis=0)

    inv_q = columns(0)
    inv_k = columns(2)
    n_keys = KB * ROWS
    slot = lax.broadcasted_iota(jnp.int32, (1, n_keys), 1)
    counts = jnp.zeros((1, n_keys), F32)
    for p in range(KB):
        line = kv_ref[p, 0:16, 4 * FEAT :][0:1].astype(F32)
        counts = jnp.where(slot // ROWS == p, jnp.concatenate([line, line], axis=1), counts)
    live = (slot % ROWS).astype(F32) < counts
    lane = lax.broadcasted_iota(jnp.int32, (QB * ROWS, 128), 1)
    stats = jnp.zeros((QB * ROWS, 128), F32)
    contract = (((1,), (1,)), ((), ()))
    extra = kv_ref[0, :, 4 * FEAT :].astype(F32)
    for h in range(HEADS):
        cols = slice(h * HEAD_DIM, (h + 1) * HEAD_DIM)

        def gain(first):
            rows = [extra[first + t * HEADS + h : first + t * HEADS + h + 1] for t in range(3)]
            return rows[0] + rows[1] + rows[2]

        def part(t):
            return kv_ref[:, :, t * FEAT + h * HEAD_DIM : t * FEAT + (h + 1) * HEAD_DIM].reshape(
                n_keys, HEAD_DIM
            )

        q = q_ref[:, :, cols].reshape(QB * ROWS, HEAD_DIM).astype(F32)
        q = (q * inv_q * gain(1)).astype(BF)
        k = (part(0).astype(F32) * inv_k * gain(10)).astype(BF)
        s1 = lax.dot_general(q, k, contract, preferred_element_type=F32) * SCALE
        s2 = lax.dot_general(q, part(2), contract, preferred_element_type=F32) * SCALE
        s2 = jnp.where(live, s2, NEGATIVE)
        peak = jnp.max(jnp.maximum(s1, s2), axis=1, keepdims=True).astype(BF).astype(F32)
        w1 = jnp.exp(s1 - peak)
        w2 = jnp.where(live, jnp.exp(s2 - peak), 0.0)
        total = jnp.sum(w1 + w2, axis=1, keepdims=True)
        mixed = jnp.dot(w1.astype(BF), part(1), preferred_element_type=F32) + jnp.dot(
            w2.astype(BF), part(3), preferred_element_type=F32
        )
        out_ref[:, h * ROWS : (h + 1) * ROWS] = (
            (mixed / total).astype(BF).reshape(QB, ROWS, HEAD_DIM)
        )
        high = total.astype(BF).astype(F32)
        stats = jnp.where(lane == h, peak, stats)
        stats = jnp.where(lane == HEADS + h, high, stats)
        stats = jnp.where(lane == 2 * HEADS + h, total - high, stats)
    for half in range(2):
        lines = stats[half * 128 : (half + 1) * 128].T[:STATS]
        for j in range(4):
            turned = lines if j == 0 else pltpu.roll(lines, 128 - j * ROWS, 1)
            out_ref[half * 4 + j, HEADS * ROWS :] = turned.astype(BF)


def project_kernel(part_ref, weight_ref, out_ref):
    stats = part_ref[:, HEADS * ROWS :].astype(F32).reshape(QB * STATS, 128).T[:ROWS]
    pieces = []
    for h in range(HEADS):

        def column(j, s):
            return stats[:, j * STATS + s * HEADS + h : j * STATS + s * HEADS + h + 1]

        peaks = [column(j, 0) for j in range(QB)]
        totals = [column(j, 1) + column(j, 2) for j in range(QB)]
        peak = peaks[0]
        for other in peaks[1:]:
            peak = jnp.maximum(peak, other)
        shares = [t * jnp.exp(m - peak) for t, m in zip(totals, peaks)]
        total = sum(shares)
        mixed = sum(
            part_ref[j, h * ROWS : (h + 1) * ROWS].astype(F32) * shares[j] for j in range(QB)
        )
        pieces.append((mixed / total).astype(BF))
    attended = jnp.concatenate(pieces, axis=1)
    for w in range(HB):
        out_ref[w] = jnp.dot(
            attended, weight_ref[:, w * WIDTH : (w + 1) * WIDTH], preferred_element_type=F32
        ).astype(BF)


def finish_kernel(step_ref, part_ref, hidden_ref, gate_ref, out_ref):
    projected = part_ref[0].astype(F32)
    for h in range(1, HB):
        projected = projected + part_ref[h].astype(F32)
    gate = gate_ref[pl.ds(step_ref[0], 1), :]
    out_ref[...] = (hidden_ref[...].astype(F32) + gate * projected).astype(BF)


def shards(
    hidden,
    query,
    key,
    value,
    query_gain,
    key_gain,
    ref_key,
    ref_value,
    ref_count,
    out_weight,
    gate_table,
    frame_step,
):
    vmem = pl.BlockSpec(memory_space=pltpu.VMEM)
    queries, block = call(
        pack_kernel,
        (
            jax.ShapeDtypeStruct((QB, ROWS, FEAT), BF),
            jax.ShapeDtypeStruct((ROWS, 4 * FEAT + 128), BF),
        ),
        ref_count,
        query_gain,
        key_gain,
        query,
        key,
        value,
        ref_key,
        ref_value,
        in_specs=[pl.BlockSpec(memory_space=pltpu.SMEM)] + [vmem] * 7,
        n_out=2,
        mib=60,
    )
    queries = lax.all_to_all(queries, QUERY_AXES, 0, 0, tiled=True)
    kv = lax.all_gather(block, KEY_AXES, axis=0)
    powers = call(power_kernel, jax.ShapeDtypeStruct((HB, 8, 128), F32), queries, kv)
    powers = lax.all_to_all(powers, HEAD_AXES, 0, 0, tiled=True)
    parts = call(
        attend_kernel,
        jax.ShapeDtypeStruct((QB, PIECE, HEAD_DIM), BF),
        queries,
        kv,
        powers,
        out_weight,
        in_specs=[vmem] * 3 + [pl.BlockSpec(memory_space=pl.ANY)],
        mib=50,
        cost=4 * 1024 * 1024,
    )
    parts = lax.all_to_all(parts, QUERY_AXES, 0, 0, tiled=True)
    projected = call(
        project_kernel,
        jax.ShapeDtypeStruct((HB, ROWS, WIDTH), BF),
        parts,
        out_weight,
        cost=6 * 1024 * 1024,
    )
    projected = lax.all_to_all(projected, HEAD_AXES, 0, 0, tiled=True)
    return call(
        finish_kernel,
        jax.ShapeDtypeStruct((ROWS, WIDTH), BF),
        frame_step,
        projected,
        hidden,
        gate_table,
        in_specs=[pl.BlockSpec(memory_space=pltpu.SMEM), vmem, vmem, vmem],
    )


def solution(mesh):
    wide = Mesh(mesh.devices.reshape(2, 4, 8, 4, 2), HEAD_AXES + SEQ_AXES)
    both = P(SEQ_AXES, HEAD_AXES)
    in_specs = (
        both,
        both,
        both,
        both,
        P(HEAD_AXES),
        P(HEAD_AXES),
        both,
        both,
        P(SEQ_AXES),
        P(HEAD_AXES, None),
        P(None, HEAD_AXES),
        P(SEQ_AXES),
    )
    return jax.shard_map(shards, mesh=wide, in_specs=in_specs, out_specs=both, check_vma=False)
```

```python
import math

import jax
import jax.numpy as jnp
from jax import lax
from jax.experimental import pallas as pl
from jax.experimental.pallas import tpu as pltpu
from jax.sharding import Mesh
from jax.sharding import PartitionSpec as P

HEAD_DIM = 128
HEADS = 3
FEAT = HEADS * HEAD_DIM
ROWS = 32
STATS = 16
PIECE = HEADS * ROWS + STATS
WIDTH = 640
ALL_FEATURES = 3072
EPSILON = 1e-06
NEGATIVE = -1e30
SCALE = 1.0 / math.sqrt(HEAD_DIM)
BF = jnp.bfloat16
F32 = jnp.float32

HEAD_AXES = ("yl", "x")
SEQ_AXES = ("z", "yh", "c")
KEY_AXES = ("yh", "c")
QUERY_AXES = "z"
QB = 8
KB = 8
HB = 8


def call(kernel, out_shape, *args, in_specs=None, n_out=1, cost=1, mib=16, scratch=()):
    vmem = pl.BlockSpec(memory_space=pltpu.VMEM)
    return pl.pallas_call(
        kernel,
        out_shape=out_shape,
        in_specs=in_specs or [vmem] * len(args),
        out_specs=vmem if n_out == 1 else [vmem] * n_out,
        scratch_shapes=scratch,
        cost_estimate=pl.CostEstimate(flops=cost, bytes_accessed=cost, transcendentals=0),
        compiler_params=pltpu.CompilerParams(vmem_limit_bytes=mib * 1024 * 1024),
    )(*args)


def pack_kernel(
    count_ref,
    frame_ref,
    gq_hbm,
    gk_hbm,
    q_hbm,
    k_hbm,
    v_hbm,
    rk_hbm,
    rv_hbm,
    qb_ref,
    kv_ref,
    step_ref,
    gq_ref,
    gk_ref,
    q_ref,
    sems,
):
    pairs = [(q_hbm, q_ref), (gq_hbm, gq_ref), (gk_hbm, gk_ref)]
    for t, ref in enumerate((k_hbm, v_hbm, rk_hbm, rv_hbm)):
        pairs.append((ref, kv_ref.at[:, t * FEAT : (t + 1) * FEAT]))
    copies = [pltpu.make_async_copy(a, b, sems.at[n]) for n, (a, b) in enumerate(pairs)]
    for copy in copies:
        copy.start()
    step_ref[...] = jnp.full((8, 128), frame_ref[0].astype(F32), F32)
    for copy in copies[:3]:
        copy.wait()
    query = q_ref[...]
    for peer in range(QB):
        qb_ref[peer] = query
    count = count_ref[0].astype(F32)
    parts = []
    for ref in (gq_ref, gk_ref):
        rest = ref[...]
        for _ in range(3):
            part = rest.astype(BF).astype(F32)
            parts += [part[h * 128 : (h + 1) * 128].reshape(1, 128) for h in range(HEADS)]
            rest = rest - part
    lines = [jnp.full((1, 128), count, F32)] + parts + [jnp.zeros((ROWS - 19, 128), F32)]
    kv_ref[:, 4 * FEAT :] = jnp.concatenate(lines, axis=0).astype(BF)
    for copy in copies[3:]:
        copy.wait()


def token_power(rows):
    wide = rows.astype(F32)
    squares = wide * wide
    part = squares[:, :128] + squares[:, 128:256] + squares[:, 256:]
    return jnp.sum(part.T, axis=0, keepdims=True)


def power_kernel(q_ref, kv_ref, out_ref):
    lines = []
    for g in range(2):
        lines.append(token_power(q_ref[g * 4 : g * 4 + 4].reshape(128, FEAT)))
    for g in range(2):
        lines.append(token_power(kv_ref[g * 4 : g * 4 + 4, :, :FEAT].reshape(128, FEAT)))
    block = jnp.concatenate(lines, axis=0)
    for peer in range(HB):
        out_ref[peer] = block


def attend_kernel(q_ref, kv_ref, pw_ref, weight_ref, out_ref):
    power = jnp.sum(pw_ref[...], axis=0) / ALL_FEATURES
    inverse = lax.rsqrt(power + EPSILON)

    def columns(first):
        tiles = [
            jnp.broadcast_to(inverse[first + g : first + g + 1], (128, 128)).T for g in range(2)
        ]
        return jnp.concatenate(tiles, axis=0)

    inv_q = columns(0)
    inv_k = columns(2)
    n_keys = KB * ROWS
    slot = lax.broadcasted_iota(jnp.int32, (1, n_keys), 1)
    counts = jnp.zeros((1, n_keys), F32)
    for p in range(KB):
        line = kv_ref[p, 0:16, 4 * FEAT :][0:1].astype(F32)
        counts = jnp.where(slot // ROWS == p, jnp.concatenate([line, line], axis=1), counts)
    live = (slot % ROWS).astype(F32) < counts
    lane = lax.broadcasted_iota(jnp.int32, (QB * ROWS, 128), 1)
    stats = jnp.zeros((QB * ROWS, 128), F32)
    contract = (((1,), (1,)), ((), ()))
    extra = kv_ref[0, :, 4 * FEAT :].astype(F32)
    for h in range(HEADS):
        cols = slice(h * HEAD_DIM, (h + 1) * HEAD_DIM)

        def gain(first):
            rows = [extra[first + t * HEADS + h : first + t * HEADS + h + 1] for t in range(3)]
            return rows[0] + rows[1] + rows[2]

        def part(t):
            return kv_ref[:, :, t * FEAT + h * HEAD_DIM : t * FEAT + (h + 1) * HEAD_DIM].reshape(
                n_keys, HEAD_DIM
            )

        q = q_ref[:, :, cols].reshape(QB * ROWS, HEAD_DIM).astype(F32)
        q = (q * inv_q * gain(1)).astype(BF)
        k = (part(0).astype(F32) * inv_k * gain(10)).astype(BF)
        s1 = lax.dot_general(q, k, contract, preferred_element_type=F32) * SCALE
        s2 = lax.dot_general(q, part(2), contract, preferred_element_type=F32) * SCALE
        s2 = jnp.where(live, s2, NEGATIVE)
        peak = jnp.max(jnp.maximum(s1, s2), axis=1, keepdims=True).astype(BF).astype(F32)
        w1 = jnp.exp(s1 - peak)
        w2 = jnp.where(live, jnp.exp(s2 - peak), 0.0)
        total = jnp.sum(w1 + w2, axis=1, keepdims=True)
        mixed = jnp.dot(w1.astype(BF), part(1), preferred_element_type=F32) + jnp.dot(
            w2.astype(BF), part(3), preferred_element_type=F32
        )
        out_ref[:, h * ROWS : (h + 1) * ROWS] = (
            (mixed / total).astype(BF).reshape(QB, ROWS, HEAD_DIM)
        )
        high = total.astype(BF).astype(F32)
        stats = jnp.where(lane == h, peak, stats)
        stats = jnp.where(lane == HEADS + h, high, stats)
        stats = jnp.where(lane == 2 * HEADS + h, total - high, stats)
    for half in range(2):
        lines = stats[half * 128 : (half + 1) * 128].T[:STATS]
        for j in range(4):
            turned = lines if j == 0 else pltpu.roll(lines, 128 - j * ROWS, 1)
            out_ref[half * 4 + j, HEADS * ROWS :] = turned.astype(BF)


def project_kernel(part_ref, weight_ref, out_ref):
    stats = part_ref[:, HEADS * ROWS :].astype(F32).reshape(QB * STATS, 128).T[:ROWS]
    pieces = []
    for h in range(HEADS):

        def column(j, s):
            return stats[:, j * STATS + s * HEADS + h : j * STATS + s * HEADS + h + 1]

        peaks = [column(j, 0) for j in range(QB)]
        totals = [column(j, 1) + column(j, 2) for j in range(QB)]
        peak = peaks[0]
        for other in peaks[1:]:
            peak = jnp.maximum(peak, other)
        shares = [t * jnp.exp(m - peak) for t, m in zip(totals, peaks)]
        total = sum(shares)
        mixed = sum(
            part_ref[j, h * ROWS : (h + 1) * ROWS].astype(F32) * shares[j] for j in range(QB)
        )
        pieces.append((mixed / total).astype(BF))
    attended = jnp.concatenate(pieces, axis=1)
    for w in range(HB):
        out_ref[w] = jnp.dot(
            attended, weight_ref[:, w * WIDTH : (w + 1) * WIDTH], preferred_element_type=F32
        ).astype(BF)


def finish_kernel(step_ref, part_ref, hidden_ref, gate_ref, out_ref):
    projected = part_ref[0].astype(F32)
    for h in range(1, HB):
        projected = projected + part_ref[h].astype(F32)
    table = gate_ref[...]
    row = lax.broadcasted_iota(jnp.int32, table.shape, 0).astype(F32)
    gate = jnp.sum(jnp.where(row == step_ref[0:1, 0:1], table, 0.0), axis=0, keepdims=True)
    out_ref[...] = (hidden_ref[...].astype(F32) + gate * projected).astype(BF)


def shards(
    hidden,
    query,
    key,
    value,
    query_gain,
    key_gain,
    ref_key,
    ref_value,
    ref_count,
    out_weight,
    gate_table,
    frame_step,
):
    vmem = pl.BlockSpec(memory_space=pltpu.VMEM)
    hbm = pl.BlockSpec(memory_space=pltpu.HBM)
    smem = pl.BlockSpec(memory_space=pltpu.SMEM)

    def pin(array):
        return pltpu.with_memory_space_constraint(array, pltpu.HBM)

    queries, block, step = call(
        pack_kernel,
        (
            jax.ShapeDtypeStruct((QB, ROWS, FEAT), BF),
            jax.ShapeDtypeStruct((ROWS, 4 * FEAT + 128), BF),
            jax.ShapeDtypeStruct((8, 128), F32),
        ),
        ref_count,
        frame_step,
        pin(query_gain),
        pin(key_gain),
        pin(query),
        pin(key),
        pin(value),
        pin(ref_key),
        pin(ref_value),
        in_specs=[smem] * 2 + [hbm] * 7,
        n_out=3,
        scratch=[
            pltpu.VMEM((FEAT,), F32),
            pltpu.VMEM((FEAT,), F32),
            pltpu.VMEM((ROWS, FEAT), BF),
            pltpu.SemaphoreType.DMA((7,)),
        ],
    )
    queries = lax.all_to_all(queries, QUERY_AXES, 0, 0, tiled=True)
    kv = lax.all_gather(block, KEY_AXES, axis=0)
    powers = call(power_kernel, jax.ShapeDtypeStruct((HB, 4, 128), F32), queries, kv)
    powers = lax.all_to_all(powers, HEAD_AXES, 0, 0, tiled=True)
    parts = call(
        attend_kernel,
        jax.ShapeDtypeStruct((QB, PIECE, HEAD_DIM), BF),
        queries,
        kv,
        powers,
        out_weight,
        in_specs=[vmem] * 3 + [pl.BlockSpec(memory_space=pl.ANY)],
        mib=50,
        cost=4 * 1024 * 1024,
    )
    parts = lax.all_to_all(parts, QUERY_AXES, 0, 0, tiled=True)
    projected = call(
        project_kernel,
        jax.ShapeDtypeStruct((HB, ROWS, WIDTH), BF),
        parts,
        out_weight,
        cost=6 * 1024 * 1024,
    )
    projected = lax.all_to_all(projected, HEAD_AXES, 0, 0, tiled=True)
    return call(
        finish_kernel,
        jax.ShapeDtypeStruct((ROWS, WIDTH), BF),
        step,
        projected,
        hidden,
        gate_table,
    )


def solution(mesh):
    wide = Mesh(mesh.devices.reshape(2, 4, 8, 4, 2), HEAD_AXES + SEQ_AXES)
    both = P(SEQ_AXES, HEAD_AXES)
    in_specs = (
        both,
        both,
        both,
        both,
        P(HEAD_AXES),
        P(HEAD_AXES),
        both,
        both,
        P(SEQ_AXES),
        P(HEAD_AXES, None),
        P(None, HEAD_AXES),
        P(SEQ_AXES),
    )
    return jax.shard_map(shards, mesh=wide, in_specs=in_specs, out_specs=both, check_vma=False)
```

```python
import math

import jax
import jax.numpy as jnp
from jax import lax
from jax.experimental import pallas as pl
from jax.experimental.pallas import tpu as pltpu
from jax.sharding import Mesh
from jax.sharding import PartitionSpec as P

HEAD_DIM = 128
HEADS = 3
FEAT = HEADS * HEAD_DIM
ROWS = 32
STATS = 16
PIECE = HEADS * ROWS + STATS
WIDTH = 640
ALL_FEATURES = 3072
EPSILON = 1e-06
NEGATIVE = -1e30
SCALE = 1.0 / math.sqrt(HEAD_DIM)
BF = jnp.bfloat16
F32 = jnp.float32

HEAD_AXES = ("yl", "x")
SEQ_AXES = ("z", "yh", "c")
KEY_AXES = ("yh", "c")
QUERY_AXES = "z"
QB = 8
KB = 8
HB = 8


def call(kernel, out_shape, *args, in_specs=None, n_out=1, cost=1, mib=16, scratch=()):
    vmem = pl.BlockSpec(memory_space=pltpu.VMEM)
    return pl.pallas_call(
        kernel,
        out_shape=out_shape,
        in_specs=in_specs or [vmem] * len(args),
        out_specs=vmem if n_out == 1 else [vmem] * n_out,
        scratch_shapes=scratch,
        cost_estimate=pl.CostEstimate(flops=cost, bytes_accessed=cost, transcendentals=0),
        compiler_params=pltpu.CompilerParams(vmem_limit_bytes=mib * 1024 * 1024),
    )(*args)


def pack_kernel(
    count_ref,
    gq_hbm,
    gk_hbm,
    q_hbm,
    k_hbm,
    v_hbm,
    rk_hbm,
    rv_hbm,
    qb_ref,
    kv_ref,
    gq_ref,
    gk_ref,
    q_ref,
    sems,
):
    pairs = [(q_hbm, q_ref), (gq_hbm, gq_ref), (gk_hbm, gk_ref)]
    for t, ref in enumerate((k_hbm, v_hbm, rk_hbm, rv_hbm)):
        pairs.append((ref, kv_ref.at[:, t * FEAT : (t + 1) * FEAT]))
    copies = [pltpu.make_async_copy(a, b, sems.at[n]) for n, (a, b) in enumerate(pairs)]
    for copy in copies:
        copy.start()
    for copy in copies[:3]:
        copy.wait()
    query = q_ref[...]
    for peer in range(QB):
        qb_ref[peer] = query
    count = count_ref[0].astype(F32)
    parts = []
    for ref in (gq_ref, gk_ref):
        rest = ref[...]
        for _ in range(3):
            part = rest.astype(BF).astype(F32)
            parts += [part[h * 128 : (h + 1) * 128].reshape(1, 128) for h in range(HEADS)]
            rest = rest - part
    lines = [jnp.full((1, 128), count, F32)] + parts + [jnp.zeros((ROWS - 19, 128), F32)]
    kv_ref[:, 4 * FEAT :] = jnp.concatenate(lines, axis=0).astype(BF)
    for copy in copies[3:]:
        copy.wait()


def token_power(rows):
    wide = rows.astype(F32)
    squares = wide * wide
    part = squares[:, :128] + squares[:, 128:256] + squares[:, 256:]
    return jnp.sum(part.T, axis=0, keepdims=True)


def power_kernel(q_ref, kv_ref, out_ref):
    lines = []
    for g in range(2):
        lines.append(token_power(q_ref[g * 4 : g * 4 + 4].reshape(128, FEAT)))
    for g in range(2):
        lines.append(token_power(kv_ref[g * 4 : g * 4 + 4, :, :FEAT].reshape(128, FEAT)))
    block = jnp.concatenate(lines, axis=0)
    for peer in range(HB):
        out_ref[peer] = block


def attend_kernel(frame_ref, q_ref, kv_ref, pw_ref, weight_ref, out_ref, step_ref):
    step_ref[...] = jnp.full((8, 128), frame_ref[0].astype(F32), F32)
    power = jnp.sum(pw_ref[...], axis=0) / ALL_FEATURES
    inverse = lax.rsqrt(power + EPSILON)

    def columns(first):
        tiles = [
            jnp.broadcast_to(inverse[first + g : first + g + 1], (128, 128)).T for g in range(2)
        ]
        return jnp.concatenate(tiles, axis=0)

    inv_q = columns(0)
    inv_k = columns(2)
    n_keys = KB * ROWS
    slot = lax.broadcasted_iota(jnp.int32, (1, n_keys), 1)
    counts = jnp.zeros((1, n_keys), F32)
    for p in range(KB):
        line = kv_ref[p, 0:16, 4 * FEAT :][0:1].astype(F32)
        counts = jnp.where(slot // ROWS == p, jnp.concatenate([line, line], axis=1), counts)
    live = (slot % ROWS).astype(F32) < counts
    lane = lax.broadcasted_iota(jnp.int32, (QB * ROWS, 128), 1)
    stats = jnp.zeros((QB * ROWS, 128), F32)
    contract = (((1,), (1,)), ((), ()))
    extra = kv_ref[0, :, 4 * FEAT :].astype(F32)
    for h in range(HEADS):
        cols = slice(h * HEAD_DIM, (h + 1) * HEAD_DIM)

        def gain(first):
            rows = [extra[first + t * HEADS + h : first + t * HEADS + h + 1] for t in range(3)]
            return rows[0] + rows[1] + rows[2]

        def part(t):
            return kv_ref[:, :, t * FEAT + h * HEAD_DIM : t * FEAT + (h + 1) * HEAD_DIM].reshape(
                n_keys, HEAD_DIM
            )

        q = q_ref[:, :, cols].reshape(QB * ROWS, HEAD_DIM).astype(F32)
        q = (q * inv_q * gain(1)).astype(BF)
        k = (part(0).astype(F32) * inv_k * gain(10)).astype(BF)
        s1 = lax.dot_general(q, k, contract, preferred_element_type=F32) * SCALE
        s2 = lax.dot_general(q, part(2), contract, preferred_element_type=F32) * SCALE
        s2 = jnp.where(live, s2, NEGATIVE)
        peak = jnp.max(jnp.maximum(s1, s2), axis=1, keepdims=True).astype(BF).astype(F32)
        w1 = jnp.exp(s1 - peak)
        w2 = jnp.where(live, jnp.exp(s2 - peak), 0.0)
        total = jnp.sum(w1 + w2, axis=1, keepdims=True)
        mixed = jnp.dot(w1.astype(BF), part(1), preferred_element_type=F32) + jnp.dot(
            w2.astype(BF), part(3), preferred_element_type=F32
        )
        out_ref[:, h * ROWS : (h + 1) * ROWS] = (
            (mixed / total).astype(BF).reshape(QB, ROWS, HEAD_DIM)
        )
        high = total.astype(BF).astype(F32)
        stats = jnp.where(lane == h, peak, stats)
        stats = jnp.where(lane == HEADS + h, high, stats)
        stats = jnp.where(lane == 2 * HEADS + h, total - high, stats)
    for half in range(2):
        lines = stats[half * 128 : (half + 1) * 128].T[:STATS]
        for j in range(4):
            turned = lines if j == 0 else pltpu.roll(lines, 128 - j * ROWS, 1)
            out_ref[half * 4 + j, HEADS * ROWS :] = turned.astype(BF)


def project_kernel(part_ref, weight_ref, out_ref):
    stats = part_ref[:, HEADS * ROWS :].astype(F32).reshape(QB * STATS, 128).T[:ROWS]
    pieces = []
    for h in range(HEADS):

        def column(j, s):
            return stats[:, j * STATS + s * HEADS + h : j * STATS + s * HEADS + h + 1]

        peaks = [column(j, 0) for j in range(QB)]
        totals = [column(j, 1) + column(j, 2) for j in range(QB)]
        peak = peaks[0]
        for other in peaks[1:]:
            peak = jnp.maximum(peak, other)
        shares = [t * jnp.exp(m - peak) for t, m in zip(totals, peaks)]
        total = sum(shares)
        mixed = sum(
            part_ref[j, h * ROWS : (h + 1) * ROWS].astype(F32) * shares[j] for j in range(QB)
        )
        pieces.append((mixed / total).astype(BF))
    attended = jnp.concatenate(pieces, axis=1)
    for w in range(HB):
        out_ref[w] = jnp.dot(
            attended, weight_ref[:, w * WIDTH : (w + 1) * WIDTH], preferred_element_type=F32
        ).astype(BF)


def finish_kernel(step_ref, part_ref, hidden_ref, gate_ref, out_ref):
    projected = part_ref[0].astype(F32)
    for h in range(1, HB):
        projected = projected + part_ref[h].astype(F32)
    table = gate_ref[...]
    row = lax.broadcasted_iota(jnp.int32, table.shape, 0).astype(F32)
    gate = jnp.sum(jnp.where(row == step_ref[0:1, 0:1], table, 0.0), axis=0, keepdims=True)
    out_ref[...] = (hidden_ref[...].astype(F32) + gate * projected).astype(BF)


def over_z(pieces):
    order = [list(range(QB))[::-1]]
    return lax.all_to_all(pieces, QUERY_AXES, 0, 0, tiled=True, axis_index_groups=order)


def shards(
    hidden,
    query,
    key,
    value,
    query_gain,
    key_gain,
    ref_key,
    ref_value,
    ref_count,
    out_weight,
    gate_table,
    frame_step,
):
    vmem = pl.BlockSpec(memory_space=pltpu.VMEM)
    hbm = pl.BlockSpec(memory_space=pltpu.HBM)
    smem = pl.BlockSpec(memory_space=pltpu.SMEM)

    def pin(array):
        return pltpu.with_memory_space_constraint(array, pltpu.HBM)

    queries, block = call(
        pack_kernel,
        (
            jax.ShapeDtypeStruct((QB, ROWS, FEAT), BF),
            jax.ShapeDtypeStruct((ROWS, 4 * FEAT + 128), BF),
        ),
        ref_count,
        pin(query_gain),
        pin(key_gain),
        pin(query),
        pin(key),
        pin(value),
        pin(ref_key),
        pin(ref_value),
        in_specs=[smem] + [hbm] * 7,
        n_out=2,
        scratch=[
            pltpu.VMEM((FEAT,), F32),
            pltpu.VMEM((FEAT,), F32),
            pltpu.VMEM((ROWS, FEAT), BF),
            pltpu.SemaphoreType.DMA((7,)),
        ],
    )
    queries = over_z(queries)
    kv = lax.all_gather(block, KEY_AXES, axis=0)
    powers = call(power_kernel, jax.ShapeDtypeStruct((HB, 4, 128), F32), queries, kv)
    powers = lax.all_to_all(powers, HEAD_AXES, 0, 0, tiled=True)
    parts, step = call(
        attend_kernel,
        (
            jax.ShapeDtypeStruct((QB, PIECE, HEAD_DIM), BF),
            jax.ShapeDtypeStruct((8, 128), F32),
        ),
        frame_step,
        queries,
        kv,
        powers,
        out_weight,
        in_specs=[smem] + [vmem] * 3 + [pl.BlockSpec(memory_space=pl.ANY)],
        n_out=2,
        mib=50,
        cost=4 * 1024 * 1024,
    )
    parts = over_z(parts)
    projected = call(
        project_kernel,
        jax.ShapeDtypeStruct((HB, ROWS, WIDTH), BF),
        parts,
        out_weight,
        cost=6 * 1024 * 1024,
    )
    projected = lax.all_to_all(projected, HEAD_AXES, 0, 0, tiled=True)
    return call(
        finish_kernel,
        jax.ShapeDtypeStruct((ROWS, WIDTH), BF),
        step,
        projected,
        hidden,
        gate_table,
    )


def solution(mesh):
    wide = Mesh(mesh.devices.reshape(2, 4, 8, 4, 2), HEAD_AXES + SEQ_AXES)
    both = P(SEQ_AXES, HEAD_AXES)
    in_specs = (
        both,
        both,
        both,
        both,
        P(HEAD_AXES),
        P(HEAD_AXES),
        both,
        both,
        P(SEQ_AXES),
        P(HEAD_AXES, None),
        P(None, HEAD_AXES),
        P(SEQ_AXES),
    )
    return jax.shard_map(shards, mesh=wide, in_specs=in_specs, out_specs=both, check_vma=False)
```

```python
import math

import jax
import jax.numpy as jnp
from jax import lax
from jax.experimental import pallas as pl
from jax.experimental.pallas import tpu as pltpu
from jax.sharding import Mesh
from jax.sharding import PartitionSpec as P

HEAD_DIM = 128
HEADS = 3
FEAT = HEADS * HEAD_DIM
ROWS = 32
STATS = 16
PIECE = HEADS * ROWS + STATS
WIDTH = 640
ALL_FEATURES = 3072
EPSILON = 1e-06
NEGATIVE = -1e30
SCALE = 1.0 / math.sqrt(HEAD_DIM)
BF = jnp.bfloat16
F32 = jnp.float32

HEAD_AXES = ("yl", "x")
SEQ_AXES = ("z", "yh", "c")
KEY_AXES = ("yh", "c")
QUERY_AXES = "z"
Z_ORDER = [0, 2, 4, 6, 1, 3, 5, 7]
HEAD_ORDER = [0, 5, 2, 7, 4, 1, 6, 3]
KEY_ORDER = [7, 6, 5, 4, 3, 2, 1, 0]
QB = 8
KB = 8
HB = 8


def call(kernel, out_shape, *args, in_specs=None, n_out=1, cost=1, mib=16, scratch=()):
    vmem = pl.BlockSpec(memory_space=pltpu.VMEM)
    return pl.pallas_call(
        kernel,
        out_shape=out_shape,
        in_specs=in_specs or [vmem] * len(args),
        out_specs=vmem if n_out == 1 else [vmem] * n_out,
        scratch_shapes=scratch,
        cost_estimate=pl.CostEstimate(flops=cost, bytes_accessed=cost, transcendentals=0),
        compiler_params=pltpu.CompilerParams(vmem_limit_bytes=mib * 1024 * 1024),
    )(*args)


def pack_kernel(
    count_ref,
    gq_hbm,
    gk_hbm,
    q_hbm,
    k_hbm,
    v_hbm,
    rk_hbm,
    rv_hbm,
    qb_ref,
    kv_ref,
    gq_ref,
    gk_ref,
    q_ref,
    sems,
):
    pairs = [(q_hbm, q_ref), (gq_hbm, gq_ref), (gk_hbm, gk_ref)]
    for t, ref in enumerate((k_hbm, v_hbm, rk_hbm, rv_hbm)):
        pairs.append((ref, kv_ref.at[:, t * FEAT : (t + 1) * FEAT]))
    copies = [pltpu.make_async_copy(a, b, sems.at[n]) for n, (a, b) in enumerate(pairs)]
    for copy in copies:
        copy.start()
    for copy in copies[:3]:
        copy.wait()
    query = q_ref[...]
    for peer in range(QB):
        qb_ref[peer] = query
    count = count_ref[0].astype(F32)
    parts = []
    for ref in (gq_ref, gk_ref):
        rest = ref[...]
        for _ in range(3):
            part = rest.astype(BF).astype(F32)
            parts += [part[h * 128 : (h + 1) * 128].reshape(1, 128) for h in range(HEADS)]
            rest = rest - part
    lines = [jnp.full((1, 128), count, F32)] + parts + [jnp.zeros((ROWS - 19, 128), F32)]
    kv_ref[:, 4 * FEAT :] = jnp.concatenate(lines, axis=0).astype(BF)
    for copy in copies[3:]:
        copy.wait()


def token_power(rows):
    wide = rows.astype(F32)
    squares = wide * wide
    part = squares[:, :128] + squares[:, 128:256] + squares[:, 256:]
    return jnp.sum(part.T, axis=0, keepdims=True)


def power_kernel(q_ref, kv_ref, out_ref):
    lines = []
    for g in range(2):
        lines.append(token_power(q_ref[g * 4 : g * 4 + 4].reshape(128, FEAT)))
    for g in range(2):
        lines.append(token_power(kv_ref[g * 4 : g * 4 + 4, :, :FEAT].reshape(128, FEAT)))
    block = jnp.concatenate(lines, axis=0)
    for peer in range(HB):
        out_ref[peer] = block


def attend_kernel(frame_ref, q_ref, kv_ref, pw_ref, weight_ref, out_ref, step_ref):
    step_ref[...] = jnp.full((8, 128), frame_ref[0].astype(F32), F32)
    power = jnp.sum(pw_ref[...], axis=0) / ALL_FEATURES
    inverse = lax.rsqrt(power + EPSILON)

    def columns(first):
        tiles = [
            jnp.broadcast_to(inverse[first + g : first + g + 1], (128, 128)).T for g in range(2)
        ]
        return jnp.concatenate(tiles, axis=0)

    inv_q = columns(0)
    inv_k = columns(2)
    n_keys = KB * ROWS
    slot = lax.broadcasted_iota(jnp.int32, (1, n_keys), 1)
    counts = jnp.zeros((1, n_keys), F32)
    for p in range(KB):
        line = kv_ref[p, 0:16, 4 * FEAT :][0:1].astype(F32)
        counts = jnp.where(slot // ROWS == p, jnp.concatenate([line, line], axis=1), counts)
    live = (slot % ROWS).astype(F32) < counts
    lane = lax.broadcasted_iota(jnp.int32, (QB * ROWS, 128), 1)
    stats = jnp.zeros((QB * ROWS, 128), F32)
    contract = (((1,), (1,)), ((), ()))
    extra = kv_ref[0, :, 4 * FEAT :].astype(F32)
    for h in range(HEADS):
        cols = slice(h * HEAD_DIM, (h + 1) * HEAD_DIM)

        def gain(first):
            rows = [extra[first + t * HEADS + h : first + t * HEADS + h + 1] for t in range(3)]
            return rows[0] + rows[1] + rows[2]

        def part(t):
            return kv_ref[:, :, t * FEAT + h * HEAD_DIM : t * FEAT + (h + 1) * HEAD_DIM].reshape(
                n_keys, HEAD_DIM
            )

        q = q_ref[:, :, cols].reshape(QB * ROWS, HEAD_DIM).astype(F32)
        q = (q * inv_q * gain(1)).astype(BF)
        k = (part(0).astype(F32) * inv_k * gain(10)).astype(BF)
        s1 = lax.dot_general(q, k, contract, preferred_element_type=F32) * SCALE
        s2 = lax.dot_general(q, part(2), contract, preferred_element_type=F32) * SCALE
        s2 = jnp.where(live, s2, NEGATIVE)
        peak = jnp.max(jnp.maximum(s1, s2), axis=1, keepdims=True).astype(BF).astype(F32)
        w1 = jnp.exp(s1 - peak)
        w2 = jnp.where(live, jnp.exp(s2 - peak), 0.0)
        total = jnp.sum(w1 + w2, axis=1, keepdims=True)
        mixed = jnp.dot(w1.astype(BF), part(1), preferred_element_type=F32) + jnp.dot(
            w2.astype(BF), part(3), preferred_element_type=F32
        )
        out_ref[:, h * ROWS : (h + 1) * ROWS] = (
            (mixed / total).astype(BF).reshape(QB, ROWS, HEAD_DIM)
        )
        high = total.astype(BF).astype(F32)
        stats = jnp.where(lane == h, peak, stats)
        stats = jnp.where(lane == HEADS + h, high, stats)
        stats = jnp.where(lane == 2 * HEADS + h, total - high, stats)
    for half in range(2):
        lines = stats[half * 128 : (half + 1) * 128].T[:STATS]
        for j in range(4):
            turned = lines if j == 0 else pltpu.roll(lines, 128 - j * ROWS, 1)
            out_ref[half * 4 + j, HEADS * ROWS :] = turned.astype(BF)


def project_kernel(part_ref, weight_ref, out_ref):
    stats = part_ref[:, HEADS * ROWS :].astype(F32).reshape(QB * STATS, 128).T[:ROWS]
    pieces = []
    for h in range(HEADS):

        def column(j, s):
            return stats[:, j * STATS + s * HEADS + h : j * STATS + s * HEADS + h + 1]

        peaks = [column(j, 0) for j in range(QB)]
        totals = [column(j, 1) + column(j, 2) for j in range(QB)]
        peak = peaks[0]
        for other in peaks[1:]:
            peak = jnp.maximum(peak, other)
        shares = [t * jnp.exp(m - peak) for t, m in zip(totals, peaks)]
        total = sum(shares)
        mixed = sum(
            part_ref[j, h * ROWS : (h + 1) * ROWS].astype(F32) * shares[j] for j in range(QB)
        )
        pieces.append((mixed / total).astype(BF))
    attended = jnp.concatenate(pieces, axis=1)
    for p, w in enumerate(HEAD_ORDER):
        out_ref[p] = jnp.dot(
            attended, weight_ref[:, w * WIDTH : (w + 1) * WIDTH], preferred_element_type=F32
        ).astype(BF)


def finish_kernel(step_ref, part_ref, hidden_ref, gate_ref, out_ref):
    projected = part_ref[0].astype(F32)
    for h in range(1, HB):
        projected = projected + part_ref[h].astype(F32)
    table = gate_ref[...]
    row = lax.broadcasted_iota(jnp.int32, table.shape, 0).astype(F32)
    gate = jnp.sum(jnp.where(row == step_ref[0:1, 0:1], table, 0.0), axis=0, keepdims=True)
    out_ref[...] = (hidden_ref[...].astype(F32) + gate * projected).astype(BF)


def exchange(pieces, axes, order):
    return lax.all_to_all(pieces, axes, 0, 0, tiled=True, axis_index_groups=[order])


def shards(
    hidden,
    query,
    key,
    value,
    query_gain,
    key_gain,
    ref_key,
    ref_value,
    ref_count,
    out_weight,
    gate_table,
    frame_step,
):
    vmem = pl.BlockSpec(memory_space=pltpu.VMEM)
    hbm = pl.BlockSpec(memory_space=pltpu.HBM)
    smem = pl.BlockSpec(memory_space=pltpu.SMEM)

    def pin(array):
        return pltpu.with_memory_space_constraint(array, pltpu.HBM)

    queries, block = call(
        pack_kernel,
        (
            jax.ShapeDtypeStruct((QB, ROWS, FEAT), BF),
            jax.ShapeDtypeStruct((ROWS, 4 * FEAT + 128), BF),
        ),
        ref_count,
        pin(query_gain),
        pin(key_gain),
        pin(query),
        pin(key),
        pin(value),
        pin(ref_key),
        pin(ref_value),
        in_specs=[smem] + [hbm] * 7,
        n_out=2,
        scratch=[
            pltpu.VMEM((FEAT,), F32),
            pltpu.VMEM((FEAT,), F32),
            pltpu.VMEM((ROWS, FEAT), BF),
            pltpu.SemaphoreType.DMA((7,)),
        ],
    )
    queries = exchange(queries, QUERY_AXES, Z_ORDER)
    kv = lax.all_gather(block, KEY_AXES, axis=0, axis_index_groups=[KEY_ORDER])
    powers = call(power_kernel, jax.ShapeDtypeStruct((HB, 4, 128), F32), queries, kv)
    powers = exchange(powers, HEAD_AXES, HEAD_ORDER)
    parts, step = call(
        attend_kernel,
        (
            jax.ShapeDtypeStruct((QB, PIECE, HEAD_DIM), BF),
            jax.ShapeDtypeStruct((8, 128), F32),
        ),
        frame_step,
        queries,
        kv,
        powers,
        out_weight,
        in_specs=[smem] + [vmem] * 3 + [pl.BlockSpec(memory_space=pl.ANY)],
        n_out=2,
        mib=50,
        cost=4 * 1024 * 1024,
    )
    parts = exchange(parts, QUERY_AXES, Z_ORDER)
    projected = call(
        project_kernel,
        jax.ShapeDtypeStruct((HB, ROWS, WIDTH), BF),
        parts,
        out_weight,
        cost=6 * 1024 * 1024,
    )
    projected = exchange(projected, HEAD_AXES, HEAD_ORDER)
    return call(
        finish_kernel,
        jax.ShapeDtypeStruct((ROWS, WIDTH), BF),
        step,
        projected,
        hidden,
        gate_table,
    )


def solution(mesh):
    wide = Mesh(mesh.devices.reshape(2, 4, 8, 4, 2), HEAD_AXES + SEQ_AXES)
    both = P(SEQ_AXES, HEAD_AXES)
    in_specs = (
        both,
        both,
        both,
        both,
        P(HEAD_AXES),
        P(HEAD_AXES),
        both,
        both,
        P(SEQ_AXES),
        P(HEAD_AXES, None),
        P(None, HEAD_AXES),
        P(SEQ_AXES),
    )
    return jax.shard_map(shards, mesh=wide, in_specs=in_specs, out_specs=both, check_vma=False)
```

```python
import math

import jax
import jax.numpy as jnp
from jax import lax
from jax.experimental import pallas as pl
from jax.experimental.pallas import tpu as pltpu
from jax.sharding import Mesh
from jax.sharding import PartitionSpec as P

HEAD_DIM = 128
HEADS = 3
FEAT = HEADS * HEAD_DIM
ROWS = 32
STATS = 16
PIECE = HEADS * ROWS + STATS
WIDTH = 640
ALL_FEATURES = 3072
EPSILON = 1e-06
NEGATIVE = -1e30
SCALE = 1.0 / math.sqrt(HEAD_DIM)
BF = jnp.bfloat16
F32 = jnp.float32

HEAD_AXES = ("yl", "x")
SEQ_AXES = ("z", "yh", "c")
KEY_AXES = ("yh", "c")
QUERY_AXES = "z"
Z_ORDER = [7, 5, 3, 1, 0, 2, 4, 6]
HEAD_ORDER = [0, 5, 2, 7, 4, 1, 6, 3]
KEY_ORDER = [0, 1, 2, 3, 4, 5, 6, 7]
QB = 8
KB = 8
HB = 8


def call(kernel, out_shape, *args, in_specs=None, n_out=1, cost=1, mib=16, scratch=()):
    vmem = pl.BlockSpec(memory_space=pltpu.VMEM)
    return pl.pallas_call(
        kernel,
        out_shape=out_shape,
        in_specs=in_specs or [vmem] * len(args),
        out_specs=vmem if n_out == 1 else [vmem] * n_out,
        scratch_shapes=scratch,
        cost_estimate=pl.CostEstimate(flops=cost, bytes_accessed=cost, transcendentals=0),
        compiler_params=pltpu.CompilerParams(vmem_limit_bytes=mib * 1024 * 1024),
    )(*args)


def pack_kernel(
    count_ref,
    gq_hbm,
    gk_hbm,
    q_hbm,
    k_hbm,
    v_hbm,
    rk_hbm,
    rv_hbm,
    qb_ref,
    kv_ref,
    gq_ref,
    gk_ref,
    q_ref,
    sems,
):
    pairs = [(q_hbm, q_ref), (gq_hbm, gq_ref), (gk_hbm, gk_ref)]
    for t, ref in enumerate((k_hbm, v_hbm, rk_hbm, rv_hbm)):
        pairs.append((ref, kv_ref.at[:, t * FEAT : (t + 1) * FEAT]))
    copies = [pltpu.make_async_copy(a, b, sems.at[n]) for n, (a, b) in enumerate(pairs)]
    for copy in copies:
        copy.start()
    for copy in copies[:3]:
        copy.wait()
    query = q_ref[...]
    for peer in range(QB):
        qb_ref[peer] = query
    count = count_ref[0].astype(F32)
    parts = []
    for ref in (gq_ref, gk_ref):
        rest = ref[...]
        for _ in range(3):
            part = rest.astype(BF).astype(F32)
            parts += [part[h * 128 : (h + 1) * 128].reshape(1, 128) for h in range(HEADS)]
            rest = rest - part
    lines = [jnp.full((1, 128), count, F32)] + parts + [jnp.zeros((ROWS - 19, 128), F32)]
    kv_ref[:, 4 * FEAT :] = jnp.concatenate(lines, axis=0).astype(BF)
    for copy in copies[3:]:
        copy.wait()


def token_power(rows):
    wide = rows.astype(F32)
    squares = wide * wide
    part = squares[:, :128] + squares[:, 128:256] + squares[:, 256:]
    return jnp.sum(part.T, axis=0, keepdims=True)


def power_kernel(q_ref, kv_ref, out_ref):
    lines = []
    for g in range(2):
        lines.append(token_power(q_ref[g * 4 : g * 4 + 4].reshape(128, FEAT)))
    for g in range(2):
        lines.append(token_power(kv_ref[g * 4 : g * 4 + 4, :, :FEAT].reshape(128, FEAT)))
    block = jnp.concatenate(lines, axis=0)
    for peer in range(HB):
        out_ref[peer] = block


def attend_kernel(frame_ref, q_ref, kv_ref, pw_ref, weight_ref, out_ref, step_ref):
    step_ref[...] = jnp.full((8, 128), frame_ref[0].astype(F32), F32)
    power = jnp.sum(pw_ref[...], axis=0) / ALL_FEATURES
    inverse = lax.rsqrt(power + EPSILON)

    def columns(first):
        tiles = [
            jnp.broadcast_to(inverse[first + g : first + g + 1], (128, 128)).T for g in range(2)
        ]
        return jnp.concatenate(tiles, axis=0)

    inv_q = columns(0)
    inv_k = columns(2)
    n_keys = KB * ROWS
    slot = lax.broadcasted_iota(jnp.int32, (1, n_keys), 1)
    counts = jnp.zeros((1, n_keys), F32)
    for p in range(KB):
        line = kv_ref[p, 0:16, 4 * FEAT :][0:1].astype(F32)
        counts = jnp.where(slot // ROWS == p, jnp.concatenate([line, line], axis=1), counts)
    live = (slot % ROWS).astype(F32) < counts
    lane = lax.broadcasted_iota(jnp.int32, (QB * ROWS, 128), 1)
    stats = jnp.zeros((QB * ROWS, 128), F32)
    contract = (((1,), (1,)), ((), ()))
    extra = kv_ref[0, :, 4 * FEAT :].astype(F32)
    for h in range(HEADS):
        cols = slice(h * HEAD_DIM, (h + 1) * HEAD_DIM)

        def gain(first):
            rows = [extra[first + t * HEADS + h : first + t * HEADS + h + 1] for t in range(3)]
            return rows[0] + rows[1] + rows[2]

        def part(t):
            return kv_ref[:, :, t * FEAT + h * HEAD_DIM : t * FEAT + (h + 1) * HEAD_DIM].reshape(
                n_keys, HEAD_DIM
            )

        q = q_ref[:, :, cols].reshape(QB * ROWS, HEAD_DIM).astype(F32)
        q = (q * inv_q * gain(1)).astype(BF)
        k = (part(0).astype(F32) * inv_k * gain(10)).astype(BF)
        s1 = lax.dot_general(q, k, contract, preferred_element_type=F32) * SCALE
        s2 = lax.dot_general(q, part(2), contract, preferred_element_type=F32) * SCALE
        s2 = jnp.where(live, s2, NEGATIVE)
        peak = jnp.max(jnp.maximum(s1, s2), axis=1, keepdims=True).astype(BF).astype(F32)
        w1 = jnp.exp(s1 - peak)
        w2 = jnp.where(live, jnp.exp(s2 - peak), 0.0)
        total = jnp.sum(w1 + w2, axis=1, keepdims=True)
        mixed = jnp.dot(w1.astype(BF), part(1), preferred_element_type=F32) + jnp.dot(
            w2.astype(BF), part(3), preferred_element_type=F32
        )
        out_ref[:, h * ROWS : (h + 1) * ROWS] = (
            (mixed / total).astype(BF).reshape(QB, ROWS, HEAD_DIM)
        )
        high = total.astype(BF).astype(F32)
        stats = jnp.where(lane == h, peak, stats)
        stats = jnp.where(lane == HEADS + h, high, stats)
        stats = jnp.where(lane == 2 * HEADS + h, total - high, stats)
    for half in range(2):
        lines = stats[half * 128 : (half + 1) * 128].T[:STATS]
        for j in range(4):
            turned = lines if j == 0 else pltpu.roll(lines, 128 - j * ROWS, 1)
            out_ref[half * 4 + j, HEADS * ROWS :] = turned.astype(BF)


def project_kernel(part_ref, weight_ref, out_ref):
    stats = part_ref[:, HEADS * ROWS :].astype(F32).reshape(QB * STATS, 128).T[:ROWS]
    pieces = []
    for h in range(HEADS):

        def column(j, s):
            return stats[:, j * STATS + s * HEADS + h : j * STATS + s * HEADS + h + 1]

        peaks = [column(j, 0) for j in range(QB)]
        totals = [column(j, 1) + column(j, 2) for j in range(QB)]
        peak = peaks[0]
        for other in peaks[1:]:
            peak = jnp.maximum(peak, other)
        shares = [t * jnp.exp(m - peak) for t, m in zip(totals, peaks)]
        total = sum(shares)
        mixed = sum(
            part_ref[j, h * ROWS : (h + 1) * ROWS].astype(F32) * shares[j] for j in range(QB)
        )
        pieces.append((mixed / total).astype(BF))
    attended = jnp.concatenate(pieces, axis=1)
    for p, w in enumerate(HEAD_ORDER):
        out_ref[p] = jnp.dot(
            attended, weight_ref[:, w * WIDTH : (w + 1) * WIDTH], preferred_element_type=F32
        ).astype(BF)


def finish_kernel(step_ref, part_ref, hidden_ref, gate_ref, out_ref):
    projected = part_ref[0].astype(F32)
    for h in range(1, HB):
        projected = projected + part_ref[h].astype(F32)
    table = gate_ref[...]
    row = lax.broadcasted_iota(jnp.int32, table.shape, 0).astype(F32)
    gate = jnp.sum(jnp.where(row == step_ref[0:1, 0:1], table, 0.0), axis=0, keepdims=True)
    out_ref[...] = (hidden_ref[...].astype(F32) + gate * projected).astype(BF)


def exchange(pieces, axes, order):
    return lax.all_to_all(pieces, axes, 0, 0, tiled=True, axis_index_groups=[order])


def shards(
    hidden,
    query,
    key,
    value,
    query_gain,
    key_gain,
    ref_key,
    ref_value,
    ref_count,
    out_weight,
    gate_table,
    frame_step,
):
    vmem = pl.BlockSpec(memory_space=pltpu.VMEM)
    hbm = pl.BlockSpec(memory_space=pltpu.HBM)
    smem = pl.BlockSpec(memory_space=pltpu.SMEM)

    def pin(array):
        return pltpu.with_memory_space_constraint(array, pltpu.HBM)

    queries, block = call(
        pack_kernel,
        (
            jax.ShapeDtypeStruct((QB, ROWS, FEAT), BF),
            jax.ShapeDtypeStruct((ROWS, 4 * FEAT + 128), BF),
        ),
        ref_count,
        pin(query_gain),
        pin(key_gain),
        pin(query),
        pin(key),
        pin(value),
        pin(ref_key),
        pin(ref_value),
        in_specs=[smem] + [hbm] * 7,
        n_out=2,
        scratch=[
            pltpu.VMEM((FEAT,), F32),
            pltpu.VMEM((FEAT,), F32),
            pltpu.VMEM((ROWS, FEAT), BF),
            pltpu.SemaphoreType.DMA((7,)),
        ],
    )
    queries = exchange(queries, QUERY_AXES, Z_ORDER)
    kv = lax.all_gather(block, KEY_AXES, axis=0, axis_index_groups=[KEY_ORDER])
    powers = call(power_kernel, jax.ShapeDtypeStruct((HB, 4, 128), F32), queries, kv)
    powers = exchange(powers, HEAD_AXES, HEAD_ORDER)
    parts, step = call(
        attend_kernel,
        (
            jax.ShapeDtypeStruct((QB, PIECE, HEAD_DIM), BF),
            jax.ShapeDtypeStruct((8, 128), F32),
        ),
        frame_step,
        queries,
        kv,
        powers,
        out_weight,
        in_specs=[smem] + [vmem] * 3 + [pl.BlockSpec(memory_space=pl.ANY)],
        n_out=2,
        mib=50,
        cost=4 * 1024 * 1024,
    )
    parts = exchange(parts, QUERY_AXES, Z_ORDER)
    projected = call(
        project_kernel,
        jax.ShapeDtypeStruct((HB, ROWS, WIDTH), BF),
        parts,
        out_weight,
        cost=6 * 1024 * 1024,
    )
    projected = exchange(projected, HEAD_AXES, HEAD_ORDER)
    return call(
        finish_kernel,
        jax.ShapeDtypeStruct((ROWS, WIDTH), BF),
        step,
        projected,
        hidden,
        gate_table,
    )


def solution(mesh):
    wide = Mesh(mesh.devices.reshape(2, 4, 8, 4, 2), HEAD_AXES + SEQ_AXES)
    both = P(SEQ_AXES, HEAD_AXES)
    in_specs = (
        both,
        both,
        both,
        both,
        P(HEAD_AXES),
        P(HEAD_AXES),
        both,
        both,
        P(SEQ_AXES),
        P(HEAD_AXES, None),
        P(None, HEAD_AXES),
        P(SEQ_AXES),
    )
    return jax.shard_map(shards, mesh=wide, in_specs=in_specs, out_specs=both, check_vma=False)
```

```python
import math

import jax
import jax.numpy as jnp
from jax import lax
from jax.experimental import pallas as pl
from jax.experimental.pallas import tpu as pltpu
from jax.sharding import Mesh
from jax.sharding import PartitionSpec as P

HEAD_DIM = 128
HEADS = 3
FEAT = HEADS * HEAD_DIM
ROWS = 32
STATS = 16
PIECE = HEADS * ROWS + STATS
WIDTH = 640
ALL_FEATURES = 3072
EPSILON = 1e-06
NEGATIVE = -1e30
SCALE = 1.0 / math.sqrt(HEAD_DIM)
BF = jnp.bfloat16
F32 = jnp.float32

HEAD_AXES = ("yl", "x")
SEQ_AXES = ("z", "yh", "c")
KEY_AXES = ("yh", "c")
QUERY_AXES = "z"
QUERY_ORDER = [0, 2, 4, 6, 1, 3, 5, 7]
PART_ORDER = [7, 5, 3, 1, 0, 2, 4, 6]
PLACE = [PART_ORDER.index(z) for z in QUERY_ORDER]
HEAD_ORDER = [0, 5, 2, 7, 4, 1, 6, 3]
KEY_ORDER = [0, 1, 2, 3, 4, 5, 6, 7]
QB = 8
KB = 8
HB = 8


def call(kernel, out_shape, *args, in_specs=None, n_out=1, cost=1, mib=16, scratch=()):
    vmem = pl.BlockSpec(memory_space=pltpu.VMEM)
    return pl.pallas_call(
        kernel,
        out_shape=out_shape,
        in_specs=in_specs or [vmem] * len(args),
        out_specs=vmem if n_out == 1 else [vmem] * n_out,
        scratch_shapes=scratch,
        cost_estimate=pl.CostEstimate(flops=cost, bytes_accessed=cost, transcendentals=0),
        compiler_params=pltpu.CompilerParams(vmem_limit_bytes=mib * 1024 * 1024),
    )(*args)


def pack_kernel(
    count_ref,
    gq_hbm,
    gk_hbm,
    q_hbm,
    k_hbm,
    v_hbm,
    rk_hbm,
    rv_hbm,
    qb_ref,
    kv_ref,
    gq_ref,
    gk_ref,
    q_ref,
    sems,
):
    pairs = [(q_hbm, q_ref), (gq_hbm, gq_ref), (gk_hbm, gk_ref)]
    for t, ref in enumerate((k_hbm, v_hbm, rk_hbm, rv_hbm)):
        pairs.append((ref, kv_ref.at[:, t * FEAT : (t + 1) * FEAT]))
    copies = [pltpu.make_async_copy(a, b, sems.at[n]) for n, (a, b) in enumerate(pairs)]
    for copy in copies:
        copy.start()
    for copy in copies[:3]:
        copy.wait()
    query = q_ref[...]
    for peer in range(QB):
        qb_ref[peer] = query
    count = count_ref[0].astype(F32)
    parts = []
    for ref in (gq_ref, gk_ref):
        rest = ref[...]
        for _ in range(3):
            part = rest.astype(BF).astype(F32)
            parts += [part[h * 128 : (h + 1) * 128].reshape(1, 128) for h in range(HEADS)]
            rest = rest - part
    lines = [jnp.full((1, 128), count, F32)] + parts + [jnp.zeros((ROWS - 19, 128), F32)]
    kv_ref[:, 4 * FEAT :] = jnp.concatenate(lines, axis=0).astype(BF)
    for copy in copies[3:]:
        copy.wait()


def token_power(rows):
    wide = rows.astype(F32)
    squares = wide * wide
    part = squares[:, :128] + squares[:, 128:256] + squares[:, 256:]
    return jnp.sum(part.T, axis=0, keepdims=True)


def power_kernel(q_ref, kv_ref, out_ref):
    lines = []
    for g in range(2):
        lines.append(token_power(q_ref[g * 4 : g * 4 + 4].reshape(128, FEAT)))
    for g in range(2):
        lines.append(token_power(kv_ref[g * 4 : g * 4 + 4, :, :FEAT].reshape(128, FEAT)))
    block = jnp.concatenate(lines, axis=0)
    for peer in range(HB):
        out_ref[peer] = block


def attend_kernel(frame_ref, q_ref, kv_ref, pw_ref, weight_ref, out_ref, step_ref):
    step_ref[...] = jnp.full((8, 128), frame_ref[0].astype(F32), F32)
    power = jnp.sum(pw_ref[...], axis=0) / ALL_FEATURES
    inverse = lax.rsqrt(power + EPSILON)

    def columns(first):
        tiles = [
            jnp.broadcast_to(inverse[first + g : first + g + 1], (128, 128)).T for g in range(2)
        ]
        return jnp.concatenate(tiles, axis=0)

    inv_q = columns(0)
    inv_k = columns(2)
    n_keys = KB * ROWS
    slot = lax.broadcasted_iota(jnp.int32, (1, n_keys), 1)
    counts = jnp.zeros((1, n_keys), F32)
    for p in range(KB):
        line = kv_ref[p, 0:16, 4 * FEAT :][0:1].astype(F32)
        counts = jnp.where(slot // ROWS == p, jnp.concatenate([line, line], axis=1), counts)
    live = (slot % ROWS).astype(F32) < counts
    lane = lax.broadcasted_iota(jnp.int32, (QB * ROWS, 128), 1)
    stats = jnp.zeros((QB * ROWS, 128), F32)
    contract = (((1,), (1,)), ((), ()))
    extra = kv_ref[0, :, 4 * FEAT :].astype(F32)
    for h in range(HEADS):
        cols = slice(h * HEAD_DIM, (h + 1) * HEAD_DIM)

        def gain(first):
            rows = [extra[first + t * HEADS + h : first + t * HEADS + h + 1] for t in range(3)]
            return rows[0] + rows[1] + rows[2]

        def part(t):
            return kv_ref[:, :, t * FEAT + h * HEAD_DIM : t * FEAT + (h + 1) * HEAD_DIM].reshape(
                n_keys, HEAD_DIM
            )

        q = q_ref[:, :, cols].reshape(QB * ROWS, HEAD_DIM).astype(F32)
        q = (q * inv_q * gain(1)).astype(BF)
        k = (part(0).astype(F32) * inv_k * gain(10)).astype(BF)
        s1 = lax.dot_general(q, k, contract, preferred_element_type=F32) * SCALE
        s2 = lax.dot_general(q, part(2), contract, preferred_element_type=F32) * SCALE
        s2 = jnp.where(live, s2, NEGATIVE)
        peak = jnp.max(jnp.maximum(s1, s2), axis=1, keepdims=True).astype(BF).astype(F32)
        w1 = jnp.exp(s1 - peak)
        w2 = jnp.where(live, jnp.exp(s2 - peak), 0.0)
        total = jnp.sum(w1 + w2, axis=1, keepdims=True)
        mixed = jnp.dot(w1.astype(BF), part(1), preferred_element_type=F32) + jnp.dot(
            w2.astype(BF), part(3), preferred_element_type=F32
        )
        mixed = (mixed / total).astype(BF)
        for p in range(QB):
            out_ref[PLACE[p], h * ROWS : (h + 1) * ROWS] = mixed[p * ROWS : (p + 1) * ROWS]
        high = total.astype(BF).astype(F32)
        stats = jnp.where(lane == h, peak, stats)
        stats = jnp.where(lane == HEADS + h, high, stats)
        stats = jnp.where(lane == 2 * HEADS + h, total - high, stats)
    for half in range(2):
        lines = stats[half * 128 : (half + 1) * 128].T[:STATS]
        for j in range(4):
            turned = lines if j == 0 else pltpu.roll(lines, 128 - j * ROWS, 1)
            out_ref[PLACE[half * 4 + j], HEADS * ROWS :] = turned.astype(BF)


def project_kernel(part_ref, weight_ref, out_ref):
    stats = part_ref[:, HEADS * ROWS :].astype(F32).reshape(QB * STATS, 128).T[:ROWS]
    pieces = []
    for h in range(HEADS):

        def column(j, s):
            return stats[:, j * STATS + s * HEADS + h : j * STATS + s * HEADS + h + 1]

        peaks = [column(j, 0) for j in range(QB)]
        totals = [column(j, 1) + column(j, 2) for j in range(QB)]
        peak = peaks[0]
        for other in peaks[1:]:
            peak = jnp.maximum(peak, other)
        shares = [t * jnp.exp(m - peak) for t, m in zip(totals, peaks)]
        total = sum(shares)
        mixed = sum(
            part_ref[j, h * ROWS : (h + 1) * ROWS].astype(F32) * shares[j] for j in range(QB)
        )
        pieces.append((mixed / total).astype(BF))
    attended = jnp.concatenate(pieces, axis=1)
    for p, w in enumerate(HEAD_ORDER):
        out_ref[p] = jnp.dot(
            attended, weight_ref[:, w * WIDTH : (w + 1) * WIDTH], preferred_element_type=F32
        ).astype(BF)


def finish_kernel(step_ref, part_ref, hidden_ref, gate_ref, out_ref):
    projected = part_ref[0].astype(F32)
    for h in range(1, HB):
        projected = projected + part_ref[h].astype(F32)
    table = gate_ref[...]
    row = lax.broadcasted_iota(jnp.int32, table.shape, 0).astype(F32)
    gate = jnp.sum(jnp.where(row == step_ref[0:1, 0:1], table, 0.0), axis=0, keepdims=True)
    out_ref[...] = (hidden_ref[...].astype(F32) + gate * projected).astype(BF)


def exchange(pieces, axes, order):
    return lax.all_to_all(pieces, axes, 0, 0, tiled=True, axis_index_groups=[order])


def shards(
    hidden,
    query,
    key,
    value,
    query_gain,
    key_gain,
    ref_key,
    ref_value,
    ref_count,
    out_weight,
    gate_table,
    frame_step,
):
    vmem = pl.BlockSpec(memory_space=pltpu.VMEM)
    hbm = pl.BlockSpec(memory_space=pltpu.HBM)
    smem = pl.BlockSpec(memory_space=pltpu.SMEM)

    def pin(array):
        return pltpu.with_memory_space_constraint(array, pltpu.HBM)

    queries, block = call(
        pack_kernel,
        (
            jax.ShapeDtypeStruct((QB, ROWS, FEAT), BF),
            jax.ShapeDtypeStruct((ROWS, 4 * FEAT + 128), BF),
        ),
        ref_count,
        pin(query_gain),
        pin(key_gain),
        pin(query),
        pin(key),
        pin(value),
        pin(ref_key),
        pin(ref_value),
        in_specs=[smem] + [hbm] * 7,
        n_out=2,
        scratch=[
            pltpu.VMEM((FEAT,), F32),
            pltpu.VMEM((FEAT,), F32),
            pltpu.VMEM((ROWS, FEAT), BF),
            pltpu.SemaphoreType.DMA((7,)),
        ],
    )
    queries = exchange(queries, QUERY_AXES, QUERY_ORDER)
    kv = lax.all_gather(block, KEY_AXES, axis=0, axis_index_groups=[KEY_ORDER])
    powers = call(power_kernel, jax.ShapeDtypeStruct((HB, 4, 128), F32), queries, kv)
    powers = exchange(powers, HEAD_AXES, HEAD_ORDER)
    parts, step = call(
        attend_kernel,
        (
            jax.ShapeDtypeStruct((QB, PIECE, HEAD_DIM), BF),
            jax.ShapeDtypeStruct((8, 128), F32),
        ),
        frame_step,
        queries,
        kv,
        powers,
        out_weight,
        in_specs=[smem] + [vmem] * 3 + [pl.BlockSpec(memory_space=pl.ANY)],
        n_out=2,
        mib=50,
        cost=4 * 1024 * 1024,
    )
    parts = exchange(parts, QUERY_AXES, PART_ORDER)
    projected = call(
        project_kernel,
        jax.ShapeDtypeStruct((HB, ROWS, WIDTH), BF),
        parts,
        out_weight,
        cost=6 * 1024 * 1024,
    )
    projected = exchange(projected, HEAD_AXES, HEAD_ORDER)
    return call(
        finish_kernel,
        jax.ShapeDtypeStruct((ROWS, WIDTH), BF),
        step,
        projected,
        hidden,
        gate_table,
    )


def solution(mesh):
    wide = Mesh(mesh.devices.reshape(2, 4, 8, 4, 2), HEAD_AXES + SEQ_AXES)
    both = P(SEQ_AXES, HEAD_AXES)
    in_specs = (
        both,
        both,
        both,
        both,
        P(HEAD_AXES),
        P(HEAD_AXES),
        both,
        both,
        P(SEQ_AXES),
        P(HEAD_AXES, None),
        P(None, HEAD_AXES),
        P(SEQ_AXES),
    )
    return jax.shard_map(shards, mesh=wide, in_specs=in_specs, out_specs=both, check_vma=False)
```

```python
import math

import jax
import jax.numpy as jnp
from jax import lax
from jax.experimental import pallas as pl
from jax.experimental.pallas import tpu as pltpu
from jax.sharding import Mesh
from jax.sharding import PartitionSpec as P

HEAD_DIM = 128
HEADS = 3
FEAT = HEADS * HEAD_DIM
ROWS = 32
STATS = 16
PIECE = HEADS * ROWS + STATS
WIDTH = 640
ALL_FEATURES = 3072
EPSILON = 1e-06
NEGATIVE = -1e30
SCALE = 1.0 / math.sqrt(HEAD_DIM)
BF = jnp.bfloat16
F32 = jnp.float32

HEAD_AXES = ("yl", "x")
SEQ_AXES = ("z", "yh", "c")
KEY_AXES = ("yh", "c")
QUERY_AXES = "z"
QUERY_ORDER = [4, 3, 5, 2, 6, 1, 7, 0]
PART_ORDER = [1, 0, 2, 4, 6, 3, 5, 7]
PLACE = [PART_ORDER.index(z) for z in QUERY_ORDER]
HEAD_ORDER = [0, 5, 2, 7, 4, 1, 6, 3]
KEY_ORDER = [0, 1, 2, 3, 4, 5, 6, 7]
QB = 8
KB = 8
HB = 8


def call(kernel, out_shape, *args, in_specs=None, n_out=1, cost=1, mib=16, scratch=()):
    vmem = pl.BlockSpec(memory_space=pltpu.VMEM)
    return pl.pallas_call(
        kernel,
        out_shape=out_shape,
        in_specs=in_specs or [vmem] * len(args),
        out_specs=vmem if n_out == 1 else [vmem] * n_out,
        scratch_shapes=scratch,
        cost_estimate=pl.CostEstimate(flops=cost, bytes_accessed=cost, transcendentals=0),
        compiler_params=pltpu.CompilerParams(vmem_limit_bytes=mib * 1024 * 1024),
    )(*args)


def pack_kernel(
    count_ref,
    gq_hbm,
    gk_hbm,
    q_hbm,
    k_hbm,
    v_hbm,
    rk_hbm,
    rv_hbm,
    qb_ref,
    kv_ref,
    gq_ref,
    gk_ref,
    q_ref,
    sems,
):
    pairs = [(q_hbm, q_ref), (gq_hbm, gq_ref), (gk_hbm, gk_ref)]
    for t, ref in enumerate((k_hbm, v_hbm, rk_hbm, rv_hbm)):
        pairs.append((ref, kv_ref.at[:, t * FEAT : (t + 1) * FEAT]))
    copies = [pltpu.make_async_copy(a, b, sems.at[n]) for n, (a, b) in enumerate(pairs)]
    for copy in copies:
        copy.start()
    for copy in copies[:3]:
        copy.wait()
    query = q_ref[...]
    for peer in range(QB):
        qb_ref[peer] = query
    count = count_ref[0].astype(F32)
    parts = []
    for ref in (gq_ref, gk_ref):
        rest = ref[...]
        for _ in range(3):
            part = rest.astype(BF).astype(F32)
            parts += [part[h * 128 : (h + 1) * 128].reshape(1, 128) for h in range(HEADS)]
            rest = rest - part
    lines = [jnp.full((1, 128), count, F32)] + parts + [jnp.zeros((ROWS - 19, 128), F32)]
    kv_ref[:, 4 * FEAT :] = jnp.concatenate(lines, axis=0).astype(BF)
    for copy in copies[3:]:
        copy.wait()


def token_power(rows):
    wide = rows.astype(F32)
    squares = wide * wide
    part = squares[:, :128] + squares[:, 128:256] + squares[:, 256:]
    return jnp.sum(part.T, axis=0, keepdims=True)


def power_kernel(q_ref, kv_ref, out_ref):
    lines = []
    for g in range(2):
        lines.append(token_power(q_ref[g * 4 : g * 4 + 4].reshape(128, FEAT)))
    for g in range(2):
        lines.append(token_power(kv_ref[g * 4 : g * 4 + 4, :, :FEAT].reshape(128, FEAT)))
    block = jnp.concatenate(lines, axis=0)
    for peer in range(HB):
        out_ref[peer] = block


def attend_kernel(frame_ref, q_ref, kv_ref, pw_ref, weight_ref, out_ref, step_ref):
    step_ref[...] = jnp.full((8, 128), frame_ref[0].astype(F32), F32)
    power = jnp.sum(pw_ref[...], axis=0) / ALL_FEATURES
    inverse = lax.rsqrt(power + EPSILON)

    def columns(first):
        tiles = [
            jnp.broadcast_to(inverse[first + g : first + g + 1], (128, 128)).T for g in range(2)
        ]
        return jnp.concatenate(tiles, axis=0)

    inv_q = columns(0)
    inv_k = columns(2)
    n_keys = KB * ROWS
    slot = lax.broadcasted_iota(jnp.int32, (1, n_keys), 1)
    counts = jnp.zeros((1, n_keys), F32)
    for p in range(KB):
        line = kv_ref[p, 0:16, 4 * FEAT :][0:1].astype(F32)
        counts = jnp.where(slot // ROWS == p, jnp.concatenate([line, line], axis=1), counts)
    live = (slot % ROWS).astype(F32) < counts
    lane = lax.broadcasted_iota(jnp.int32, (QB * ROWS, 128), 1)
    stats = jnp.zeros((QB * ROWS, 128), F32)
    contract = (((1,), (1,)), ((), ()))
    extra = kv_ref[0, :, 4 * FEAT :].astype(F32)
    for h in range(HEADS):
        cols = slice(h * HEAD_DIM, (h + 1) * HEAD_DIM)

        def gain(first):
            rows = [extra[first + t * HEADS + h : first + t * HEADS + h + 1] for t in range(3)]
            return rows[0] + rows[1] + rows[2]

        def part(t):
            return kv_ref[:, :, t * FEAT + h * HEAD_DIM : t * FEAT + (h + 1) * HEAD_DIM].reshape(
                n_keys, HEAD_DIM
            )

        q = q_ref[:, :, cols].reshape(QB * ROWS, HEAD_DIM).astype(F32)
        q = (q * inv_q * gain(1)).astype(BF)
        k = (part(0).astype(F32) * inv_k * gain(10)).astype(BF)
        s1 = lax.dot_general(q, k, contract, preferred_element_type=F32) * SCALE
        s2 = lax.dot_general(q, part(2), contract, preferred_element_type=F32) * SCALE
        s2 = jnp.where(live, s2, NEGATIVE)
        peak = jnp.max(jnp.maximum(s1, s2), axis=1, keepdims=True).astype(BF).astype(F32)
        w1 = jnp.exp(s1 - peak)
        w2 = jnp.where(live, jnp.exp(s2 - peak), 0.0)
        total = jnp.sum(w1 + w2, axis=1, keepdims=True)
        mixed = jnp.dot(w1.astype(BF), part(1), preferred_element_type=F32) + jnp.dot(
            w2.astype(BF), part(3), preferred_element_type=F32
        )
        mixed = (mixed / total).astype(BF)
        for p in range(QB):
            out_ref[PLACE[p], h * ROWS : (h + 1) * ROWS] = mixed[p * ROWS : (p + 1) * ROWS]
        high = total.astype(BF).astype(F32)
        stats = jnp.where(lane == h, peak, stats)
        stats = jnp.where(lane == HEADS + h, high, stats)
        stats = jnp.where(lane == 2 * HEADS + h, total - high, stats)
    for half in range(2):
        lines = stats[half * 128 : (half + 1) * 128].T[:STATS]
        for j in range(4):
            turned = lines if j == 0 else pltpu.roll(lines, 128 - j * ROWS, 1)
            out_ref[PLACE[half * 4 + j], HEADS * ROWS :] = turned.astype(BF)


def project_kernel(part_ref, weight_ref, out_ref):
    stats = part_ref[:, HEADS * ROWS :].astype(F32).reshape(QB * STATS, 128).T[:ROWS]
    pieces = []
    for h in range(HEADS):

        def column(j, s):
            return stats[:, j * STATS + s * HEADS + h : j * STATS + s * HEADS + h + 1]

        peaks = [column(j, 0) for j in range(QB)]
        totals = [column(j, 1) + column(j, 2) for j in range(QB)]
        peak = peaks[0]
        for other in peaks[1:]:
            peak = jnp.maximum(peak, other)
        shares = [t * jnp.exp(m - peak) for t, m in zip(totals, peaks)]
        total = sum(shares)
        mixed = sum(
            part_ref[j, h * ROWS : (h + 1) * ROWS].astype(F32) * shares[j] for j in range(QB)
        )
        pieces.append((mixed / total).astype(BF))
    attended = jnp.concatenate(pieces, axis=1)
    for p, w in enumerate(HEAD_ORDER):
        out_ref[p] = jnp.dot(
            attended, weight_ref[:, w * WIDTH : (w + 1) * WIDTH], preferred_element_type=F32
        ).astype(BF)


def finish_kernel(step_ref, part_ref, hidden_ref, gate_ref, out_ref):
    projected = part_ref[0].astype(F32)
    for h in range(1, HB):
        projected = projected + part_ref[h].astype(F32)
    table = gate_ref[...]
    row = lax.broadcasted_iota(jnp.int32, table.shape, 0).astype(F32)
    gate = jnp.sum(jnp.where(row == step_ref[0:1, 0:1], table, 0.0), axis=0, keepdims=True)
    out_ref[...] = (hidden_ref[...].astype(F32) + gate * projected).astype(BF)


def exchange(pieces, axes, order):
    return lax.all_to_all(pieces, axes, 0, 0, tiled=True, axis_index_groups=[order])


def shards(
    hidden,
    query,
    key,
    value,
    query_gain,
    key_gain,
    ref_key,
    ref_value,
    ref_count,
    out_weight,
    gate_table,
    frame_step,
):
    vmem = pl.BlockSpec(memory_space=pltpu.VMEM)
    hbm = pl.BlockSpec(memory_space=pltpu.HBM)
    smem = pl.BlockSpec(memory_space=pltpu.SMEM)

    def pin(array):
        return pltpu.with_memory_space_constraint(array, pltpu.HBM)

    queries, block = call(
        pack_kernel,
        (
            jax.ShapeDtypeStruct((QB, ROWS, FEAT), BF),
            jax.ShapeDtypeStruct((ROWS, 4 * FEAT + 128), BF),
        ),
        ref_count,
        pin(query_gain),
        pin(key_gain),
        pin(query),
        pin(key),
        pin(value),
        pin(ref_key),
        pin(ref_value),
        in_specs=[smem] + [hbm] * 7,
        n_out=2,
        scratch=[
            pltpu.VMEM((FEAT,), F32),
            pltpu.VMEM((FEAT,), F32),
            pltpu.VMEM((ROWS, FEAT), BF),
            pltpu.SemaphoreType.DMA((7,)),
        ],
    )
    queries = exchange(queries, QUERY_AXES, QUERY_ORDER)
    kv = lax.all_gather(block, KEY_AXES, axis=0, axis_index_groups=[KEY_ORDER])
    powers = call(power_kernel, jax.ShapeDtypeStruct((HB, 4, 128), F32), queries, kv)
    powers = exchange(powers, HEAD_AXES, HEAD_ORDER)
    parts, step = call(
        attend_kernel,
        (
            jax.ShapeDtypeStruct((QB, PIECE, HEAD_DIM), BF),
            jax.ShapeDtypeStruct((8, 128), F32),
        ),
        frame_step,
        queries,
        kv,
        powers,
        out_weight,
        in_specs=[smem] + [vmem] * 3 + [pl.BlockSpec(memory_space=pl.ANY)],
        n_out=2,
        mib=50,
        cost=4 * 1024 * 1024,
    )
    parts = exchange(parts, QUERY_AXES, PART_ORDER)
    projected = call(
        project_kernel,
        jax.ShapeDtypeStruct((HB, ROWS, WIDTH), BF),
        parts,
        out_weight,
        cost=6 * 1024 * 1024,
    )
    projected = exchange(projected, HEAD_AXES, HEAD_ORDER)
    return call(
        finish_kernel,
        jax.ShapeDtypeStruct((ROWS, WIDTH), BF),
        step,
        projected,
        hidden,
        gate_table,
    )


def solution(mesh):
    wide = Mesh(mesh.devices.reshape(2, 4, 8, 4, 2), HEAD_AXES + SEQ_AXES)
    both = P(SEQ_AXES, HEAD_AXES)
    in_specs = (
        both,
        both,
        both,
        both,
        P(HEAD_AXES),
        P(HEAD_AXES),
        both,
        both,
        P(SEQ_AXES),
        P(HEAD_AXES, None),
        P(None, HEAD_AXES),
        P(SEQ_AXES),
    )
    return jax.shard_map(shards, mesh=wide, in_specs=in_specs, out_specs=both, check_vma=False)
```

```python
import math

import jax
import jax.numpy as jnp
from jax import lax
from jax.experimental import pallas as pl
from jax.experimental.pallas import tpu as pltpu
from jax.sharding import Mesh
from jax.sharding import PartitionSpec as P

HEAD_DIM = 128
HEADS = 3
FEAT = HEADS * HEAD_DIM
ROWS = 32
STATS = 16
PIECE = HEADS * ROWS + STATS
WIDTH = 640
ALL_FEATURES = 3072
EPSILON = 1e-06
NEGATIVE = -1e30
SCALE = 1.0 / math.sqrt(HEAD_DIM)
BF = jnp.bfloat16
F32 = jnp.float32

HEAD_AXES = ("yl", "x")
SEQ_AXES = ("z", "yh", "c")
KEY_AXES = ("yh", "c")
QUERY_AXES = "z"
QUERY_ORDER = [4, 5, 3, 6, 2, 7, 1, 0]
PART_ORDER = [1, 0, 2, 4, 6, 3, 5, 7]
PLACE = [PART_ORDER.index(z) for z in QUERY_ORDER]
HEAD_ORDER = [0, 5, 2, 7, 4, 1, 6, 3]
KEY_ORDER = [0, 1, 2, 3, 4, 5, 6, 7]
QB = 8
KB = 8
HB = 8


def call(kernel, out_shape, *args, in_specs=None, out_specs=None, n_out=1, cost=1, mib=16, scratch=()):
    vmem = pl.BlockSpec(memory_space=pltpu.VMEM)
    return pl.pallas_call(
        kernel,
        out_shape=out_shape,
        in_specs=in_specs or [vmem] * len(args),
        out_specs=out_specs or (vmem if n_out == 1 else [vmem] * n_out),
        scratch_shapes=scratch,
        cost_estimate=pl.CostEstimate(flops=cost, bytes_accessed=cost, transcendentals=0),
        compiler_params=pltpu.CompilerParams(vmem_limit_bytes=mib * 1024 * 1024),
    )(*args)


def pack_kernel(
    count_ref,
    gq_hbm,
    gk_hbm,
    q_hbm,
    k_hbm,
    v_hbm,
    rk_hbm,
    rv_hbm,
    qb_hbm,
    kv_ref,
    gq_ref,
    gk_ref,
    q_ref,
    sems,
):
    pairs = [(q_hbm, q_ref), (gq_hbm, gq_ref), (gk_hbm, gk_ref)]
    for t, ref in enumerate((k_hbm, v_hbm, rk_hbm, rv_hbm)):
        pairs.append((ref, kv_ref.at[:, t * FEAT : (t + 1) * FEAT]))
    copies = [pltpu.make_async_copy(a, b, sems.at[n]) for n, (a, b) in enumerate(pairs)]
    for copy in copies:
        copy.start()
    copies[0].wait()
    spread = [
        pltpu.make_async_copy(q_ref, qb_hbm.at[peer], sems.at[7 + peer]) for peer in range(QB)
    ]
    for copy in spread:
        copy.start()
    for copy in copies[1:3]:
        copy.wait()
    count = count_ref[0].astype(F32)
    parts = []
    for ref in (gq_ref, gk_ref):
        rest = ref[...]
        for _ in range(3):
            part = rest.astype(BF).astype(F32)
            parts += [part[h * 128 : (h + 1) * 128].reshape(1, 128) for h in range(HEADS)]
            rest = rest - part
    lines = [jnp.full((1, 128), count, F32)] + parts + [jnp.zeros((ROWS - 19, 128), F32)]
    kv_ref[:, 4 * FEAT :] = jnp.concatenate(lines, axis=0).astype(BF)
    for copy in copies[3:] + spread:
        copy.wait()


def token_power(rows):
    wide = rows.astype(F32)
    squares = wide * wide
    part = squares[:, :128] + squares[:, 128:256] + squares[:, 256:]
    return jnp.sum(part.T, axis=0, keepdims=True)


def power_kernel(q_ref, kv_ref, out_ref):
    lines = []
    for g in range(2):
        lines.append(token_power(q_ref[g * 4 : g * 4 + 4].reshape(128, FEAT)))
    for g in range(2):
        lines.append(token_power(kv_ref[g * 4 : g * 4 + 4, :, :FEAT].reshape(128, FEAT)))
    block = jnp.concatenate(lines, axis=0)
    for peer in range(HB):
        out_ref[peer] = block


def attend_kernel(frame_ref, q_ref, kv_ref, pw_ref, weight_ref, out_ref, step_ref):
    step_ref[...] = jnp.full((8, 128), frame_ref[0].astype(F32), F32)
    power = jnp.sum(pw_ref[...], axis=0) / ALL_FEATURES
    inverse = lax.rsqrt(power + EPSILON)

    def columns(first):
        tiles = [
            jnp.broadcast_to(inverse[first + g : first + g + 1], (128, 128)).T for g in range(2)
        ]
        return jnp.concatenate(tiles, axis=0)

    inv_q = columns(0)
    inv_k = columns(2)
    n_keys = KB * ROWS
    slot = lax.broadcasted_iota(jnp.int32, (1, n_keys), 1)
    counts = jnp.zeros((1, n_keys), F32)
    for p in range(KB):
        line = kv_ref[p, 0:16, 4 * FEAT :][0:1].astype(F32)
        counts = jnp.where(slot // ROWS == p, jnp.concatenate([line, line], axis=1), counts)
    live = (slot % ROWS).astype(F32) < counts
    lane = lax.broadcasted_iota(jnp.int32, (QB * ROWS, 128), 1)
    stats = jnp.zeros((QB * ROWS, 128), F32)
    contract = (((1,), (1,)), ((), ()))
    extra = kv_ref[0, :, 4 * FEAT :].astype(F32)
    for h in range(HEADS):
        cols = slice(h * HEAD_DIM, (h + 1) * HEAD_DIM)

        def gain(first):
            rows = [extra[first + t * HEADS + h : first + t * HEADS + h + 1] for t in range(3)]
            return rows[0] + rows[1] + rows[2]

        def part(t):
            return kv_ref[:, :, t * FEAT + h * HEAD_DIM : t * FEAT + (h + 1) * HEAD_DIM].reshape(
                n_keys, HEAD_DIM
            )

        q = q_ref[:, :, cols].reshape(QB * ROWS, HEAD_DIM).astype(F32)
        q = (q * inv_q * gain(1)).astype(BF)
        k = (part(0).astype(F32) * inv_k * gain(10)).astype(BF)
        s1 = lax.dot_general(q, k, contract, preferred_element_type=F32) * SCALE
        s2 = lax.dot_general(q, part(2), contract, preferred_element_type=F32) * SCALE
        s2 = jnp.where(live, s2, NEGATIVE)
        peak = jnp.max(jnp.maximum(s1, s2), axis=1, keepdims=True).astype(BF).astype(F32)
        w1 = jnp.exp(s1 - peak)
        w2 = jnp.where(live, jnp.exp(s2 - peak), 0.0)
        total = jnp.sum(w1 + w2, axis=1, keepdims=True)
        mixed = jnp.dot(w1.astype(BF), part(1), preferred_element_type=F32) + jnp.dot(
            w2.astype(BF), part(3), preferred_element_type=F32
        )
        mixed = (mixed / total).astype(BF)
        for p in range(QB):
            out_ref[PLACE[p], h * ROWS : (h + 1) * ROWS] = mixed[p * ROWS : (p + 1) * ROWS]
        high = total.astype(BF).astype(F32)
        stats = jnp.where(lane == h, peak, stats)
        stats = jnp.where(lane == HEADS + h, high, stats)
        stats = jnp.where(lane == 2 * HEADS + h, total - high, stats)
    for half in range(2):
        lines = stats[half * 128 : (half + 1) * 128].T[:STATS]
        for j in range(4):
            turned = lines if j == 0 else pltpu.roll(lines, 128 - j * ROWS, 1)
            out_ref[PLACE[half * 4 + j], HEADS * ROWS :] = turned.astype(BF)


def project_kernel(part_ref, weight_ref, out_ref):
    stats = part_ref[:, HEADS * ROWS :].astype(F32).reshape(QB * STATS, 128).T[:ROWS]
    pieces = []
    for h in range(HEADS):

        def column(j, s):
            return stats[:, j * STATS + s * HEADS + h : j * STATS + s * HEADS + h + 1]

        peaks = [column(j, 0) for j in range(QB)]
        totals = [column(j, 1) + column(j, 2) for j in range(QB)]
        peak = peaks[0]
        for other in peaks[1:]:
            peak = jnp.maximum(peak, other)
        shares = [t * jnp.exp(m - peak) for t, m in zip(totals, peaks)]
        total = sum(shares)
        mixed = sum(
            part_ref[j, h * ROWS : (h + 1) * ROWS].astype(F32) * shares[j] for j in range(QB)
        )
        pieces.append((mixed / total).astype(BF))
    attended = jnp.concatenate(pieces, axis=1)
    for p, w in enumerate(HEAD_ORDER):
        out_ref[p] = jnp.dot(
            attended, weight_ref[:, w * WIDTH : (w + 1) * WIDTH], preferred_element_type=F32
        ).astype(BF)


def finish_kernel(step_ref, part_ref, hidden_ref, gate_ref, out_ref):
    projected = part_ref[0].astype(F32)
    for h in range(1, HB):
        projected = projected + part_ref[h].astype(F32)
    table = gate_ref[...]
    row = lax.broadcasted_iota(jnp.int32, table.shape, 0).astype(F32)
    gate = jnp.sum(jnp.where(row == step_ref[0:1, 0:1], table, 0.0), axis=0, keepdims=True)
    out_ref[...] = (hidden_ref[...].astype(F32) + gate * projected).astype(BF)


def exchange(pieces, axes, order):
    return lax.all_to_all(pieces, axes, 0, 0, tiled=True, axis_index_groups=[order])


def shards(
    hidden,
    query,
    key,
    value,
    query_gain,
    key_gain,
    ref_key,
    ref_value,
    ref_count,
    out_weight,
    gate_table,
    frame_step,
):
    vmem = pl.BlockSpec(memory_space=pltpu.VMEM)
    hbm = pl.BlockSpec(memory_space=pltpu.HBM)
    smem = pl.BlockSpec(memory_space=pltpu.SMEM)

    def pin(array):
        return pltpu.with_memory_space_constraint(array, pltpu.HBM)

    queries, block = call(
        pack_kernel,
        (
            jax.ShapeDtypeStruct((QB, ROWS, FEAT), BF),
            jax.ShapeDtypeStruct((ROWS, 4 * FEAT + 128), BF),
        ),
        ref_count,
        pin(query_gain),
        pin(key_gain),
        pin(query),
        pin(key),
        pin(value),
        pin(ref_key),
        pin(ref_value),
        in_specs=[smem] + [hbm] * 7,
        out_specs=[hbm, vmem],
        scratch=[
            pltpu.VMEM((FEAT,), F32),
            pltpu.VMEM((FEAT,), F32),
            pltpu.VMEM((ROWS, FEAT), BF),
            pltpu.SemaphoreType.DMA((7 + QB,)),
        ],
    )
    queries = exchange(queries, QUERY_AXES, QUERY_ORDER)
    kv = lax.all_gather(block, KEY_AXES, axis=0, axis_index_groups=[KEY_ORDER])
    powers = call(power_kernel, jax.ShapeDtypeStruct((HB, 4, 128), F32), queries, kv)
    powers = exchange(powers, HEAD_AXES, HEAD_ORDER)
    parts, step = call(
        attend_kernel,
        (
            jax.ShapeDtypeStruct((QB, PIECE, HEAD_DIM), BF),
            jax.ShapeDtypeStruct((8, 128), F32),
        ),
        frame_step,
        queries,
        kv,
        powers,
        out_weight,
        in_specs=[smem] + [vmem] * 3 + [pl.BlockSpec(memory_space=pl.ANY)],
        n_out=2,
        mib=50,
        cost=4 * 1024 * 1024,
    )
    parts = exchange(parts, QUERY_AXES, PART_ORDER)
    projected = call(
        project_kernel,
        jax.ShapeDtypeStruct((HB, ROWS, WIDTH), BF),
        parts,
        out_weight,
        cost=6 * 1024 * 1024,
    )
    projected = exchange(projected, HEAD_AXES, HEAD_ORDER)
    return call(
        finish_kernel,
        jax.ShapeDtypeStruct((ROWS, WIDTH), BF),
        step,
        projected,
        hidden,
        gate_table,
    )


def solution(mesh):
    wide = Mesh(mesh.devices.reshape(2, 4, 8, 4, 2), HEAD_AXES + SEQ_AXES)
    both = P(SEQ_AXES, HEAD_AXES)
    in_specs = (
        both,
        both,
        both,
        both,
        P(HEAD_AXES),
        P(HEAD_AXES),
        both,
        both,
        P(SEQ_AXES),
        P(HEAD_AXES, None),
        P(None, HEAD_AXES),
        P(SEQ_AXES),
    )
    return jax.shard_map(shards, mesh=wide, in_specs=in_specs, out_specs=both, check_vma=False)
```

```python
import math

import jax
import jax.numpy as jnp
from jax import lax
from jax.experimental import pallas as pl
from jax.experimental.pallas import tpu as pltpu
from jax.sharding import Mesh
from jax.sharding import PartitionSpec as P

HEAD_DIM = 128
HEADS = 3
FEAT = HEADS * HEAD_DIM
ROWS = 32
STATS = 16
PIECE = HEADS * ROWS + STATS
WIDTH = 640
ALL_FEATURES = 3072
EPSILON = 1e-06
NEGATIVE = -1e30
SCALE = 1.0 / math.sqrt(HEAD_DIM)
BF = jnp.bfloat16
F32 = jnp.float32

HEAD_AXES = ("yl", "x")
SEQ_AXES = ("z", "yh", "c")
KEY_AXES = ("yh", "c")
QUERY_AXES = "z"
QUERY_ORDER = [4, 5, 3, 6, 2, 7, 1, 0]
PART_ORDER = [1, 0, 2, 4, 6, 3, 5, 7]
PLACE = [PART_ORDER.index(z) for z in QUERY_ORDER]
HEAD_ORDER = [0, 5, 2, 7, 4, 1, 6, 3]
KEY_ORDER = [7, 6, 5, 4, 3, 2, 1, 0]
QB = 8
KB = 8
HB = 8


def call(kernel, out_shape, *args, in_specs=None, out_specs=None, n_out=1, cost=1, mib=16, scratch=()):
    vmem = pl.BlockSpec(memory_space=pltpu.VMEM)
    return pl.pallas_call(
        kernel,
        out_shape=out_shape,
        in_specs=in_specs or [vmem] * len(args),
        out_specs=out_specs or (vmem if n_out == 1 else [vmem] * n_out),
        scratch_shapes=scratch,
        cost_estimate=pl.CostEstimate(flops=cost, bytes_accessed=cost, transcendentals=0),
        compiler_params=pltpu.CompilerParams(vmem_limit_bytes=mib * 1024 * 1024),
    )(*args)


def pack_kernel(
    count_ref,
    gq_hbm,
    gk_hbm,
    q_hbm,
    k_hbm,
    v_hbm,
    rk_hbm,
    rv_hbm,
    qb_hbm,
    kv_ref,
    gq_ref,
    gk_ref,
    q_ref,
    sems,
):
    pairs = [(q_hbm, q_ref), (gq_hbm, gq_ref), (gk_hbm, gk_ref)]
    for t, ref in enumerate((k_hbm, v_hbm, rk_hbm, rv_hbm)):
        pairs.append((ref, kv_ref.at[:, t * FEAT : (t + 1) * FEAT]))
    copies = [pltpu.make_async_copy(a, b, sems.at[n]) for n, (a, b) in enumerate(pairs)]
    for copy in copies:
        copy.start()
    copies[0].wait()
    spread = [
        pltpu.make_async_copy(q_ref, qb_hbm.at[peer], sems.at[7 + peer]) for peer in range(QB)
    ]
    for copy in spread:
        copy.start()
    for copy in copies[1:3]:
        copy.wait()
    count = count_ref[0].astype(F32)
    parts = []
    for ref in (gq_ref, gk_ref):
        rest = ref[...]
        for _ in range(3):
            part = rest.astype(BF).astype(F32)
            parts += [part[h * 128 : (h + 1) * 128].reshape(1, 128) for h in range(HEADS)]
            rest = rest - part
    lines = [jnp.full((1, 128), count, F32)] + parts + [jnp.zeros((ROWS - 19, 128), F32)]
    kv_ref[:, 4 * FEAT :] = jnp.concatenate(lines, axis=0).astype(BF)
    for copy in copies[3:] + spread:
        copy.wait()


def token_power(rows):
    wide = rows.astype(F32)
    squares = wide * wide
    part = squares[:, :128] + squares[:, 128:256] + squares[:, 256:]
    return jnp.sum(part.T, axis=0, keepdims=True)


def power_kernel(q_ref, kv_ref, out_ref):
    lines = []
    for g in range(2):
        lines.append(token_power(q_ref[g * 4 : g * 4 + 4].reshape(128, FEAT)))
    for g in range(2):
        lines.append(token_power(kv_ref[g * 4 : g * 4 + 4, :, :FEAT].reshape(128, FEAT)))
    block = jnp.concatenate(lines, axis=0)
    for peer in range(HB):
        out_ref[peer] = block


def attend_kernel(frame_ref, q_ref, kv_ref, pw_ref, weight_ref, out_ref, step_ref):
    step_ref[...] = jnp.full((8, 128), frame_ref[0].astype(F32), F32)
    power = jnp.sum(pw_ref[...], axis=0) / ALL_FEATURES
    inverse = lax.rsqrt(power + EPSILON)

    def columns(first):
        tiles = [
            jnp.broadcast_to(inverse[first + g : first + g + 1], (128, 128)).T for g in range(2)
        ]
        return jnp.concatenate(tiles, axis=0)

    inv_q = columns(0)
    inv_k = columns(2)
    n_keys = KB * ROWS
    slot = lax.broadcasted_iota(jnp.int32, (1, n_keys), 1)
    counts = jnp.zeros((1, n_keys), F32)
    for p in range(KB):
        line = kv_ref[p, 0:16, 4 * FEAT :][0:1].astype(F32)
        counts = jnp.where(slot // ROWS == p, jnp.concatenate([line, line], axis=1), counts)
    live = (slot % ROWS).astype(F32) < counts
    lane = lax.broadcasted_iota(jnp.int32, (QB * ROWS, 128), 1)
    stats = jnp.zeros((QB * ROWS, 128), F32)
    contract = (((1,), (1,)), ((), ()))
    extra = kv_ref[0, :, 4 * FEAT :].astype(F32)
    for h in range(HEADS):
        cols = slice(h * HEAD_DIM, (h + 1) * HEAD_DIM)

        def gain(first):
            rows = [extra[first + t * HEADS + h : first + t * HEADS + h + 1] for t in range(3)]
            return rows[0] + rows[1] + rows[2]

        def part(t):
            return kv_ref[:, :, t * FEAT + h * HEAD_DIM : t * FEAT + (h + 1) * HEAD_DIM].reshape(
                n_keys, HEAD_DIM
            )

        q = q_ref[:, :, cols].reshape(QB * ROWS, HEAD_DIM).astype(F32)
        q = (q * inv_q * gain(1)).astype(BF)
        k = (part(0).astype(F32) * inv_k * gain(10)).astype(BF)
        s1 = lax.dot_general(q, k, contract, preferred_element_type=F32) * SCALE
        s2 = lax.dot_general(q, part(2), contract, preferred_element_type=F32) * SCALE
        s2 = jnp.where(live, s2, NEGATIVE)
        peak = jnp.max(jnp.maximum(s1, s2), axis=1, keepdims=True).astype(BF).astype(F32)
        w1 = jnp.exp(s1 - peak)
        w2 = jnp.where(live, jnp.exp(s2 - peak), 0.0)
        total = jnp.sum(w1 + w2, axis=1, keepdims=True)
        mixed = jnp.dot(w1.astype(BF), part(1), preferred_element_type=F32) + jnp.dot(
            w2.astype(BF), part(3), preferred_element_type=F32
        )
        mixed = (mixed / total).astype(BF)
        for p in range(QB):
            out_ref[PLACE[p], h * ROWS : (h + 1) * ROWS] = mixed[p * ROWS : (p + 1) * ROWS]
        high = total.astype(BF).astype(F32)
        stats = jnp.where(lane == h, peak, stats)
        stats = jnp.where(lane == HEADS + h, high, stats)
        stats = jnp.where(lane == 2 * HEADS + h, total - high, stats)
    for half in range(2):
        lines = stats[half * 128 : (half + 1) * 128].T[:STATS]
        for j in range(4):
            turned = lines if j == 0 else pltpu.roll(lines, 128 - j * ROWS, 1)
            out_ref[PLACE[half * 4 + j], HEADS * ROWS :] = turned.astype(BF)


def project_kernel(part_ref, weight_ref, out_ref):
    stats = part_ref[:, HEADS * ROWS :].astype(F32).reshape(QB * STATS, 128).T[:ROWS]
    pieces = []
    for h in range(HEADS):

        def column(j, s):
            return stats[:, j * STATS + s * HEADS + h : j * STATS + s * HEADS + h + 1]

        peaks = [column(j, 0) for j in range(QB)]
        totals = [column(j, 1) + column(j, 2) for j in range(QB)]
        peak = peaks[0]
        for other in peaks[1:]:
            peak = jnp.maximum(peak, other)
        shares = [t * jnp.exp(m - peak) for t, m in zip(totals, peaks)]
        total = sum(shares)
        mixed = sum(
            part_ref[j, h * ROWS : (h + 1) * ROWS].astype(F32) * shares[j] for j in range(QB)
        )
        pieces.append((mixed / total).astype(BF))
    attended = jnp.concatenate(pieces, axis=1)
    for p, w in enumerate(HEAD_ORDER):
        out_ref[p] = jnp.dot(
            attended, weight_ref[:, w * WIDTH : (w + 1) * WIDTH], preferred_element_type=F32
        ).astype(BF)


def finish_kernel(step_ref, part_ref, hidden_ref, gate_ref, out_ref):
    projected = part_ref[0].astype(F32)
    for h in range(1, HB):
        projected = projected + part_ref[h].astype(F32)
    table = gate_ref[...]
    row = lax.broadcasted_iota(jnp.int32, table.shape, 0).astype(F32)
    gate = jnp.sum(jnp.where(row == step_ref[0:1, 0:1], table, 0.0), axis=0, keepdims=True)
    out_ref[...] = (hidden_ref[...].astype(F32) + gate * projected).astype(BF)


def exchange(pieces, axes, order):
    return lax.all_to_all(pieces, axes, 0, 0, tiled=True, axis_index_groups=[order])


def shards(
    hidden,
    query,
    key,
    value,
    query_gain,
    key_gain,
    ref_key,
    ref_value,
    ref_count,
    out_weight,
    gate_table,
    frame_step,
):
    vmem = pl.BlockSpec(memory_space=pltpu.VMEM)
    hbm = pl.BlockSpec(memory_space=pltpu.HBM)
    smem = pl.BlockSpec(memory_space=pltpu.SMEM)

    def pin(array):
        return pltpu.with_memory_space_constraint(array, pltpu.HBM)

    queries, block = call(
        pack_kernel,
        (
            jax.ShapeDtypeStruct((QB, ROWS, FEAT), BF),
            jax.ShapeDtypeStruct((ROWS, 4 * FEAT + 128), BF),
        ),
        ref_count,
        pin(query_gain),
        pin(key_gain),
        pin(query),
        pin(key),
        pin(value),
        pin(ref_key),
        pin(ref_value),
        in_specs=[smem] + [hbm] * 7,
        out_specs=[hbm, vmem],
        scratch=[
            pltpu.VMEM((FEAT,), F32),
            pltpu.VMEM((FEAT,), F32),
            pltpu.VMEM((ROWS, FEAT), BF),
            pltpu.SemaphoreType.DMA((7 + QB,)),
        ],
    )
    queries = exchange(queries, QUERY_AXES, QUERY_ORDER)
    kv = lax.all_gather(block, KEY_AXES, axis=0, axis_index_groups=[KEY_ORDER])
    powers = call(power_kernel, jax.ShapeDtypeStruct((HB, 4, 128), F32), queries, kv)
    powers = exchange(powers, HEAD_AXES, HEAD_ORDER)
    parts, step = call(
        attend_kernel,
        (
            jax.ShapeDtypeStruct((QB, PIECE, HEAD_DIM), BF),
            jax.ShapeDtypeStruct((8, 128), F32),
        ),
        frame_step,
        queries,
        kv,
        powers,
        out_weight,
        in_specs=[smem] + [vmem] * 3 + [pl.BlockSpec(memory_space=pl.ANY)],
        n_out=2,
        mib=50,
        cost=4 * 1024 * 1024,
    )
    parts = exchange(parts, QUERY_AXES, PART_ORDER)
    projected = call(
        project_kernel,
        jax.ShapeDtypeStruct((HB, ROWS, WIDTH), BF),
        parts,
        out_weight,
        cost=6 * 1024 * 1024,
    )
    projected = exchange(projected, HEAD_AXES, HEAD_ORDER)
    return call(
        finish_kernel,
        jax.ShapeDtypeStruct((ROWS, WIDTH), BF),
        step,
        projected,
        hidden,
        gate_table,
    )


def solution(mesh):
    wide = Mesh(mesh.devices.reshape(2, 4, 8, 4, 2), HEAD_AXES + SEQ_AXES)
    both = P(SEQ_AXES, HEAD_AXES)
    in_specs = (
        both,
        both,
        both,
        both,
        P(HEAD_AXES),
        P(HEAD_AXES),
        both,
        both,
        P(SEQ_AXES),
        P(HEAD_AXES, None),
        P(None, HEAD_AXES),
        P(SEQ_AXES),
    )
    return jax.shard_map(shards, mesh=wide, in_specs=in_specs, out_specs=both, check_vma=False)
```
